256 devices in a mesh: src: 32 (over x, z), tgt: 8 (over y, core).
Axes of the slice: x: 4, y: 4, z: 8, core: 2. Of those that a mesh axis runs over, the one named last changes fastest.
Arguments:
- src_points: float32 [16384, 32], P(('src', 'tgt')), may hold values from -4.5 to 4.5
- log_a: float32 [16384], P(('src', 'tgt')), may hold values from -1 to 1
- tgt_points: float32 [65536, 32], P(('src', 'tgt')), may hold values from -1.5 to 1.5
- log_b: float32 [65536], P(('src', 'tgt')), may hold values from -1 to 1
- g_init: float32 [65536], P(('src', 'tgt')), may hold values from -60 to 1.5
Outputs:
- f_pot: float32 [16384], P(('src', 'tgt'))
- g_pot: float32 [65536], P(('src', 'tgt'))
The draws below stay inside these ranges and needn't reach their ends.
All inputs are finite; a program needn't handle non-finite values.
Results may differ from the reference program's by a relative error of at most 0.0003.
Values sent between devices are 32-bit elements; how exact they have to be, the bound alone decides.
No kernel may reach another device: no remote copies, remote signals or barrier semaphores. Data moves between devices by JAX's collectives and lax.ppermute only.
A program may use at most 64 MiB of HBM per device.

```python
import jax
import jax.numpy as jnp
from jax import lax

DIM = 32
ITERS = 2
NS = 16384
NT = 65536


def outlier_rows(key):
    period = min(4096, NT)
    first_key, second_key = jax.random.split(jax.random.fold_in(key, 97))
    offset = jax.random.randint(first_key, (), 0, period)
    row_index = jnp.arange(NT, dtype=jnp.int32)
    chosen = (row_index + offset) % period == 0
    corner_signs = jax.random.randint(second_key, (NT, DIM), 0, 2).astype(jnp.float32) * 2.0 - 1.0
    return (chosen, corner_signs)


def draw_src_points(key, part):
    key = jax.random.fold_in(key, 11)
    first = jax.random.fold_in(key, 0)
    return jnp.clip(0.25 * jax.random.normal(first, (NS, DIM), jnp.float32), -1.5, 1.5)


def draw_tgt_points(key, part):
    chosen, corner_signs = outlier_rows(key)
    key = jax.random.fold_in(key, 12)
    base = jnp.clip(0.25 * jax.random.normal(key, (NT, DIM), jnp.float32), -1.5, 1.5)
    return jnp.where(chosen[:, None], 1.5 * corner_signs, base)


def draw_log_b(key, part):
    chosen, corner_signs = outlier_rows(key)
    key = jax.random.fold_in(key, 13)
    base = jax.random.uniform(key, (NT,), jnp.float32, -1.0, 1.0)
    return jnp.where(chosen, -1.0, base)


def draw_g_init(key, part):
    chosen, corner_signs = outlier_rows(key)
    key = jax.random.fold_in(key, 14)
    base = jnp.clip(0.5 * jax.random.normal(key, (NT,), jnp.float32), -1.5, 1.5)
    return jnp.where(chosen, -60.0, base)


def shard_levels(key, shape, pieces, low, largest):
    level = 1.0
    for position, parts in pieces:
        heights = jax.random.uniform(jax.random.fold_in(jax.random.fold_in(key, 6), position), (parts,), jnp.float32, low / len(pieces), largest / len(pieces))
        level = level * jnp.repeat(jnp.exp(heights), shape[position] // parts).reshape((-1,) + (1,) * (len(shape) - 1 - position))
    return level


def setup_inputs(seed: int = 0) -> dict:
    key_list = jax.random.split(jax.random.key(seed), 6)
    src_points = draw_src_points(jax.random.fold_in(key_list[5], 71), 0)
    log_a = jnp.clip(jax.random.uniform(key_list[1], (NS,), jnp.float32, -1.0, 1.0) * shard_levels(key_list[1], (NS,), ((0, 256),), -0.4, 0.0), -1.0, 1.0)
    tgt_points = draw_tgt_points(jax.random.fold_in(key_list[5], 71), 0)
    log_b = draw_log_b(jax.random.fold_in(key_list[5], 71), 0)
    g_init = draw_g_init(jax.random.fold_in(key_list[5], 71), 0)
    return dict(src_points=src_points, log_a=log_a, tgt_points=tgt_points, log_b=log_b, g_init=g_init)


EPSILON = 0.5


def distance_block(sources, targets, target_sq):
    source_sq = jnp.sum(sources * sources, axis=1)
    cross = lax.dot_general(sources, targets, (((1,), (1,)), ((), ())), precision=lax.Precision.HIGHEST, preferred_element_type=jnp.float32)
    return source_sq[:, None] + target_sq[None, :] - 2.0 * cross


def reference(src_points, log_a, tgt_points, log_b, g_init):
    block = min(512, NS)
    count = NS // block
    target_sq = jnp.sum(tgt_points * tgt_points, axis=1)
    source_blocks = src_points.reshape(count, block, DIM)
    weight_blocks = log_a.reshape(count, block)
    g_now = g_init
    f_now = jnp.zeros((NS,), jnp.float32)
    for sweep in range(ITERS):
        def row_pass(sources, g_cur=g_now):
            dist = distance_block(sources, tgt_points, target_sq)
            terms = log_b[None, :] + (g_cur[None, :] - dist) / EPSILON
            top = jnp.max(terms, axis=1)
            return -EPSILON * (top + jnp.log(jnp.sum(jnp.exp(terms - top[:, None]), axis=1)))

        f_now = lax.map(row_pass, source_blocks).reshape(NS)
        f_blocks = f_now.reshape(count, block)

        def column_pass(carry, inputs):
            top, total = carry
            sources, weights, f_part = inputs
            dist = distance_block(sources, tgt_points, target_sq)
            terms = weights[:, None] + (f_part[:, None] - dist) / EPSILON
            newtop = jnp.maximum(top, jnp.max(terms, axis=0))
            total = total * jnp.exp(top - newtop) + jnp.sum(jnp.exp(terms - newtop[None, :]), axis=0)
            return (newtop, total), None

        start = (jnp.full((NT,), -1e30, jnp.float32), jnp.zeros((NT,), jnp.float32))
        (top, total), unused = lax.scan(column_pass, start, (source_blocks, weight_blocks, f_blocks))
        g_now = -EPSILON * (top + jnp.log(total))
    return f_now, g_now
```

```python
import functools

import jax
import jax.numpy as jnp
import numpy as np
from jax import lax
from jax.experimental import pallas as pl
from jax.experimental.pallas import tpu as pltpu
from jax.sharding import Mesh
from jax.sharding import PartitionSpec as P

EPSILON = 0.5
LOG2E = float(np.log2(np.e))
LN2 = float(np.log(2.0))
AXES = ("x", "z", "y", "c")
SOURCE_AXES = ("z", "c")
TARGET_AXES = ("x", "y")
DIM = 32
DEPTH = 128
VEC = 3 * DIM
TILE = 256
CHUNK = 64
F32 = jnp.float32
BF16 = jnp.bfloat16
PARAMS = pltpu.CompilerParams(vmem_limit_bytes=48 << 20)


def split(v, count):
    pieces = []
    for _ in range(count):
        piece = v.astype(BF16)
        pieces.append(piece.astype(F32))
        v = v - pieces[-1]
    return pieces


def vector_rows(first, second, width):
    def rows(v):
        if v is None:
            return [jnp.ones((1, width), F32)] * 3
        return split(v, 3)

    zeros = jnp.zeros((10, width), F32)
    return jnp.concatenate(rows(first) + rows(second) + [zeros], axis=0).astype(BF16)


def combine(parts):
    top = jnp.max(parts, axis=0)
    return top + jnp.log2(jnp.sum(jnp.exp2(parts - top[None]), axis=0))


def lse_pass(lhs_ref, rhs_ref, write):
    chunks = lhs_ref.shape[0] // CHUNK

    def tile(n, carry):
        rhs = rhs_ref[:, pl.ds(pl.multiple_of(n * TILE, TILE), TILE)]

        def step(r, state):
            top, total = state
            lhs = lhs_ref[pl.ds(pl.multiple_of(r * CHUNK, CHUNK), CHUNK), :]
            terms = jnp.dot(lhs, rhs, preferred_element_type=F32).reshape(CHUNK // 8, 8, TILE)
            newtop = jnp.maximum(top, jnp.max(terms, axis=0))
            added = jnp.sum(jnp.exp2(terms - newtop[None]), axis=0)
            return newtop, total * jnp.exp2(top - newtop) + added

        start = (jnp.full((8, TILE), -1e30, F32), jnp.zeros((8, TILE), F32))
        top, total = lax.fori_loop(0, chunks, step, start, unroll=16)
        peak = jnp.max(top, axis=0, keepdims=True)
        total = jnp.sum(total * jnp.exp2(top - peak), axis=0, keepdims=True)
        write(n, peak + jnp.log2(total))
        return carry

    lax.fori_loop(0, rhs_ref.shape[1] // TILE, tile, 0)


def write_copies(out_ref):
    def write(n, value):
        at = pl.ds(pl.multiple_of(n * TILE, TILE), TILE)
        out_ref[:, :, at] = jnp.broadcast_to(value[None], (out_ref.shape[0], 1, TILE))

    return write


def pack_kernel(src, la, tgt, lb, g, spack, tpack, ssq, tsq):
    s_t = src[...].T
    t_t = tgt[...].T
    s_norm = jnp.sum(s_t * s_t, axis=0, keepdims=True)
    t_norm = jnp.sum(t_t * t_t, axis=0, keepdims=True)
    ssq[...] = s_norm
    tsq[...] = t_norm
    s_t = s_t * ((2.0 / EPSILON) * LOG2E)
    half = DIM // 2
    weights = jnp.concatenate([la[...] * LOG2E, jnp.zeros_like(la[...])], axis=1)
    packed = jnp.concatenate(
        [jnp.concatenate([s_t[:half], s_t[half:]], axis=1), jnp.broadcast_to(weights, (8, weights.shape[1]))], axis=0
    )
    spack[...] = jnp.broadcast_to(packed[None], spack.shape)
    h = (lb[...] + (g[...] - t_norm) / EPSILON) * LOG2E
    rest = jnp.concatenate([h, lb[...] * LOG2E, jnp.zeros((6, h.shape[1]), F32)], axis=0)
    tpack[...] = jnp.broadcast_to(jnp.concatenate([t_t, rest], axis=0)[None], tpack.shape)


def first_kernel(spg, tpg, out, akm, bkm, la, lb, brm, bh):
    groups, _, lanes = spg.shape
    half = DIM // 2
    own = lanes // 2
    pieces = []
    for p in range(0, groups, 2):
        a, b = spg[p], spg[p + 1]
        top = jnp.concatenate([a[:, :own], b[:, :own]], axis=1)
        low = jnp.concatenate([a[:half, own:], b[:half, own:]], axis=1)
        la[:, own * p : own * (p + 2)] = top[half : half + 1]
        pieces.append(jnp.concatenate([top[:half], low], axis=0))
    s = jnp.concatenate(pieces, axis=1)
    s1, s2 = (v.astype(BF16) for v in split(s, 2))
    width = s.shape[1]
    none = jnp.zeros((1, width), F32)
    akm[...] = jnp.concatenate([s1, s1, s2, vector_rows(none, None, width), jnp.zeros((16, width), BF16)], axis=0)
    width = tpg.shape[2]
    none = jnp.zeros((1, width), F32)
    for p in range(tpg.shape[0]):
        at = slice(width * p, width * (p + 1))
        t1, t2 = (v.astype(BF16) for v in split(tpg[p, :DIM], 2))
        h = tpg[p, DIM : DIM + 1]
        lb[:, at] = tpg[p, DIM + 1 : DIM + 2]
        zeros = jnp.zeros((16, width), BF16)
        bkm[:, at] = jnp.concatenate([t1, t2, t1, vector_rows(None, none, width), zeros], axis=0)
        bh[...] = jnp.concatenate([t1, t2, t1, vector_rows(None, h, width), zeros], axis=0)
        brm[at, :] = bh[...].T
    lse_pass(brm, akm, write_copies(out))


def column_kernel(parts, la, akm, bkm, out, arm, tmp):
    k = la[...] - combine(parts[...])
    tmp[...] = akm[...]
    tmp[VEC : VEC + 16, :] = vector_rows(k, None, k.shape[1])
    arm[...] = tmp[...].T
    lse_pass(arm, bkm, write_copies(out))


def row_kernel(parts, lb, akm, bkm, out, brm, tmp):
    h = lb[...] - combine(parts[...])
    tmp[...] = bkm[...]
    tmp[VEC : VEC + 16, :] = vector_rows(None, h, h.shape[1])
    brm[...] = tmp[...].T
    lse_pass(brm, akm, write_copies(out))


def last_column_kernel(parts, la, akm, bkm, ssq, out, f, arm, tmp):
    rows = combine(parts[...])
    me = lax.axis_index(TARGET_AXES)
    own = f.shape[1]
    mine = jnp.zeros((1, own), F32)
    for p in range(rows.shape[1] // own):
        mine = mine + jnp.where(me == p, rows[:, own * p : own * (p + 1)], 0.0)
    f[...] = ssq[...] - (EPSILON * LN2) * mine
    k = la[...] - rows
    tmp[...] = akm[...]
    tmp[VEC : VEC + 16, :] = vector_rows(k, None, k.shape[1])
    arm[...] = tmp[...].T

    def write(n, value):
        out[n] = value

    lse_pass(arm, bkm, write)


def last_kernel(parts, tsq, g):
    g[...] = tsq[...] - (EPSILON * LN2) * combine(parts[...])


def call(kernel, name, outs, *args, scratch=()):
    whole = pl.BlockSpec(memory_space=pltpu.VMEM)
    return pl.pallas_call(
        kernel,
        name=name,
        out_shape=[jax.ShapeDtypeStruct(*o) for o in outs],
        in_specs=[whole] * len(args),
        out_specs=[whole] * len(outs),
        scratch_shapes=list(scratch),
        compiler_params=PARAMS,
    )(*args)


def exchange(v, axes):
    return lax.all_to_all(v, axes, 0, 0, tiled=True)


def local(src_points, log_a, tgt_points, log_b, g_init):
    own_s, own_t = src_points.shape[0], tgt_points.shape[0]
    across_t = lax.axis_size(TARGET_AXES)
    across_s = lax.axis_size(SOURCE_AXES)
    rows, cols = own_s * across_t, own_t * across_s
    row = lambda v: v.reshape(1, -1)
    spack, tpack, ssq, tsq = call(
        pack_kernel,
        "pack",
        [
            ((across_t, DIM // 2 + 8, 2 * own_s), F32),
            ((across_s, DIM + 8, own_t), F32),
            ((1, own_s), F32),
            ((1, own_t), F32),
        ],
        src_points,
        row(log_a),
        tgt_points,
        row(log_b),
        row(g_init),
    )
    spg = exchange(spack, TARGET_AXES)
    tpg = exchange(tpack, SOURCE_AXES)
    row_out = ((across_t, 1, rows), F32)
    col_out = ((across_s, 1, cols), F32)
    parts, akm, bkm, la, lb = call(
        first_kernel,
        "row_pass_first",
        [row_out, ((DEPTH, rows), BF16), ((DEPTH, cols), BF16), ((1, rows), F32), ((1, cols), F32)],
        spg,
        tpg,
        scratch=[pltpu.VMEM((cols, DEPTH), BF16), pltpu.VMEM((DEPTH, own_t), BF16)],
    )
    row_scratch = [pltpu.VMEM((cols, DEPTH), BF16), pltpu.VMEM((DEPTH, cols), BF16)]
    col_scratch = [pltpu.VMEM((rows, DEPTH), BF16), pltpu.VMEM((DEPTH, rows), BF16)]
    parts = exchange(parts, TARGET_AXES)
    (parts,) = call(column_kernel, "column_pass", [col_out], parts, la, akm, bkm, scratch=col_scratch)
    parts = exchange(parts, SOURCE_AXES)
    (parts,) = call(row_kernel, "row_pass", [row_out], parts, lb, akm, bkm, scratch=row_scratch)
    parts = exchange(parts, TARGET_AXES)
    parts, f = call(
        last_column_kernel,
        "column_pass_last",
        [((across_s, 1, own_t), F32), ((1, own_s), F32)],
        parts,
        la,
        akm,
        bkm,
        ssq,
        scratch=col_scratch,
    )
    parts = exchange(parts, SOURCE_AXES)
    (g,) = call(last_kernel, "last", [((1, own_t), F32)], parts, tsq)
    return f.reshape(own_s), g.reshape(own_t)


def solution(mesh):
    fine = Mesh(mesh.devices.reshape(4, 8, 4, 2), AXES)
    flat = P(AXES)
    return jax.shard_map(
        local,
        mesh=fine,
        in_specs=(P(AXES, None), flat, P(AXES, None), flat, flat),
        out_specs=(flat, flat),
        check_vma=False,
    )
```

```python
import functools

import jax
import jax.numpy as jnp
import numpy as np
from jax import lax
from jax.experimental import pallas as pl
from jax.experimental.pallas import tpu as pltpu
from jax.sharding import Mesh
from jax.sharding import PartitionSpec as P

EPSILON = 0.5
LOG2E = float(np.log2(np.e))
LN2 = float(np.log(2.0))
AXES = ("x", "z", "y", "c")
SOURCE_AXES = ("x", "y")
TARGET_AXES = ("z", "c")
DIM = 32
DEPTH = 128
VEC = 3 * DIM
TILE = 512
CHUNK = 128
F32 = jnp.float32
BF16 = jnp.bfloat16
PARAMS = pltpu.CompilerParams(vmem_limit_bytes=48 << 20)


def split(v, count):
    pieces = []
    for _ in range(count):
        piece = v.astype(BF16)
        pieces.append(piece.astype(F32))
        v = v - pieces[-1]
    return pieces


def vector_rows(first, second, width):
    def rows(v):
        if v is None:
            return [jnp.ones((1, width), F32)] * 3
        return split(v, 3)

    zeros = jnp.zeros((10, width), F32)
    return jnp.concatenate(rows(first) + rows(second) + [zeros], axis=0).astype(BF16)


def combine(parts):
    top = jnp.max(parts, axis=0)
    return top + jnp.log2(jnp.sum(jnp.exp2(parts - top[None]), axis=0))


def lse_pass(lhs_ref, rhs_ref, write):
    for at in range(0, rhs_ref.shape[1], TILE):
        rhs = rhs_ref[:, at : at + TILE]
        top = total = None
        for row in range(0, lhs_ref.shape[0], CHUNK):
            terms = jnp.dot(lhs_ref[row : row + CHUNK, :], rhs, preferred_element_type=F32)
            terms = terms.reshape(CHUNK // 8, 8, TILE)
            newtop = jnp.max(terms, axis=0)
            if top is not None:
                newtop = jnp.maximum(top, newtop)
            added = jnp.sum(jnp.exp2(terms - newtop[None]), axis=0)
            total = added if top is None else total * jnp.exp2(top - newtop) + added
            top = newtop
        peak = jnp.max(top, axis=0, keepdims=True)
        total = jnp.sum(total * jnp.exp2(top - peak), axis=0, keepdims=True)
        write(at, peak + jnp.log2(total))


def write_copies(out_ref):
    def write(at, value):
        out_ref[:, :, at : at + TILE] = jnp.broadcast_to(value[None], (out_ref.shape[0], 1, TILE))

    return write


def pack_kernel(src, la, tgt, lb, g, spack, tpack, ssq, tsq):
    s_t = src[...].T
    t_t = tgt[...].T
    s_norm = jnp.sum(s_t * s_t, axis=0, keepdims=True)
    t_norm = jnp.sum(t_t * t_t, axis=0, keepdims=True)
    ssq[...] = s_norm
    tsq[...] = t_norm
    s_t = s_t * ((2.0 / EPSILON) * LOG2E)
    half = DIM // 2
    weights = jnp.concatenate([la[...] * LOG2E, jnp.zeros_like(la[...])], axis=1)
    packed = jnp.concatenate(
        [jnp.concatenate([s_t[:half], s_t[half:]], axis=1), jnp.broadcast_to(weights, (8, weights.shape[1]))], axis=0
    )
    spack[...] = jnp.broadcast_to(packed[None], spack.shape)
    h = (lb[...] + (g[...] - t_norm) / EPSILON) * LOG2E
    rest = jnp.concatenate([h, lb[...] * LOG2E, jnp.zeros((6, h.shape[1]), F32)], axis=0)
    tpack[...] = jnp.broadcast_to(jnp.concatenate([t_t, rest], axis=0)[None], tpack.shape)


def first_kernel(spg, tpg, out, akm, bkm, la, lb, brm, bh):
    groups, _, lanes = spg.shape
    half = DIM // 2
    own = lanes // 2
    pieces = []
    for p in range(0, groups, 2):
        a, b = spg[p], spg[p + 1]
        top = jnp.concatenate([a[:, :own], b[:, :own]], axis=1)
        low = jnp.concatenate([a[:half, own:], b[:half, own:]], axis=1)
        la[:, own * p : own * (p + 2)] = top[half : half + 1]
        pieces.append(jnp.concatenate([top[:half], low], axis=0))
    s = jnp.concatenate(pieces, axis=1)
    s1, s2 = (v.astype(BF16) for v in split(s, 2))
    width = s.shape[1]
    none = jnp.zeros((1, width), F32)
    akm[...] = jnp.concatenate([s1, s1, s2, vector_rows(none, None, width), jnp.zeros((16, width), BF16)], axis=0)
    width = tpg.shape[2]
    none = jnp.zeros((1, width), F32)
    for p in range(tpg.shape[0]):
        at = slice(width * p, width * (p + 1))
        t1, t2 = (v.astype(BF16) for v in split(tpg[p, :DIM], 2))
        h = tpg[p, DIM : DIM + 1]
        lb[:, at] = tpg[p, DIM + 1 : DIM + 2]
        zeros = jnp.zeros((16, width), BF16)
        bkm[:, at] = jnp.concatenate([t1, t2, t1, vector_rows(None, none, width), zeros], axis=0)
        bh[...] = jnp.concatenate([t1, t2, t1, vector_rows(None, h, width), zeros], axis=0)
        brm[at, :] = bh[...].T
    lse_pass(brm, akm, write_copies(out))


def column_kernel(parts, la, akm, bkm, out, arm, tmp):
    k = la[...] - combine(parts[...])
    tmp[...] = akm[...]
    tmp[VEC : VEC + 16, :] = vector_rows(k, None, k.shape[1])
    arm[...] = tmp[...].T
    lse_pass(arm, bkm, write_copies(out))


def row_kernel(parts, lb, akm, bkm, out, brm, tmp):
    h = lb[...] - combine(parts[...])
    tmp[...] = bkm[...]
    tmp[VEC : VEC + 16, :] = vector_rows(None, h, h.shape[1])
    brm[...] = tmp[...].T
    lse_pass(brm, akm, write_copies(out))


def last_column_kernel(parts, la, akm, bkm, ssq, out, f, arm, tmp):
    rows = combine(parts[...])
    me = lax.axis_index(TARGET_AXES)
    own = f.shape[1]
    mine = jnp.zeros((1, own), F32)
    for p in range(rows.shape[1] // own):
        mine = mine + jnp.where(me == p, rows[:, own * p : own * (p + 1)], 0.0)
    f[...] = ssq[...] - (EPSILON * LN2) * mine
    k = la[...] - rows
    tmp[...] = akm[...]
    tmp[VEC : VEC + 16, :] = vector_rows(k, None, k.shape[1])
    arm[...] = tmp[...].T

    def write(at, value):
        for own in range(0, TILE, out.shape[2]):
            out[(at + own) // out.shape[2]] = value[:, own : own + out.shape[2]]

    lse_pass(arm, bkm, write)


def last_kernel(parts, tsq, g):
    g[...] = tsq[...] - (EPSILON * LN2) * combine(parts[...])


def call(kernel, name, outs, *args, scratch=()):
    whole = pl.BlockSpec(memory_space=pltpu.VMEM)
    return pl.pallas_call(
        kernel,
        name=name,
        out_shape=[jax.ShapeDtypeStruct(*o) for o in outs],
        in_specs=[whole] * len(args),
        out_specs=[whole] * len(outs),
        scratch_shapes=list(scratch),
        compiler_params=PARAMS,
    )(*args)


def exchange(v, axes):
    return lax.all_to_all(v, axes, 0, 0, tiled=True)


def local(src_points, log_a, tgt_points, log_b, g_init):
    own_s, own_t = src_points.shape[0], tgt_points.shape[0]
    across_t = lax.axis_size(TARGET_AXES)
    across_s = lax.axis_size(SOURCE_AXES)
    rows, cols = own_s * across_t, own_t * across_s
    row = lambda v: v.reshape(1, -1)
    spack, tpack, ssq, tsq = call(
        pack_kernel,
        "pack",
        [
            ((across_t, DIM // 2 + 8, 2 * own_s), F32),
            ((across_s, DIM + 8, own_t), F32),
            ((1, own_s), F32),
            ((1, own_t), F32),
        ],
        src_points,
        row(log_a),
        tgt_points,
        row(log_b),
        row(g_init),
    )
    spg = exchange(spack, TARGET_AXES)
    tpg = exchange(tpack, SOURCE_AXES)
    row_out = ((across_t, 1, rows), F32)
    col_out = ((across_s, 1, cols), F32)
    parts, akm, bkm, la, lb = call(
        first_kernel,
        "row_pass_first",
        [row_out, ((DEPTH, rows), BF16), ((DEPTH, cols), BF16), ((1, rows), F32), ((1, cols), F32)],
        spg,
        tpg,
        scratch=[pltpu.VMEM((cols, DEPTH), BF16), pltpu.VMEM((DEPTH, own_t), BF16)],
    )
    row_scratch = [pltpu.VMEM((cols, DEPTH), BF16), pltpu.VMEM((DEPTH, cols), BF16)]
    col_scratch = [pltpu.VMEM((rows, DEPTH), BF16), pltpu.VMEM((DEPTH, rows), BF16)]
    parts = exchange(parts, TARGET_AXES)
    (parts,) = call(column_kernel, "column_pass", [col_out], parts, la, akm, bkm, scratch=col_scratch)
    parts = exchange(parts, SOURCE_AXES)
    (parts,) = call(row_kernel, "row_pass", [row_out], parts, lb, akm, bkm, scratch=row_scratch)
    parts = exchange(parts, TARGET_AXES)
    parts, f = call(
        last_column_kernel,
        "column_pass_last",
        [((across_s, 1, own_t), F32), ((1, own_s), F32)],
        parts,
        la,
        akm,
        bkm,
        ssq,
        scratch=col_scratch,
    )
    parts = exchange(parts, SOURCE_AXES)
    (g,) = call(last_kernel, "last", [((1, own_t), F32)], parts, tsq)
    return f.reshape(own_s), g.reshape(own_t)


def solution(mesh):
    fine = Mesh(mesh.devices.reshape(4, 8, 4, 2), AXES)
    flat = P(AXES)
    return jax.shard_map(
        local,
        mesh=fine,
        in_specs=(P(AXES, None), flat, P(AXES, None), flat, flat),
        out_specs=(flat, flat),
        check_vma=False,
    )
```

```python
import functools

import jax
import jax.numpy as jnp
import numpy as np
from jax import lax
from jax.experimental import pallas as pl
from jax.experimental.pallas import tpu as pltpu
from jax.sharding import Mesh
from jax.sharding import PartitionSpec as P

EPSILON = 0.5
LOG2E = float(np.log2(np.e))
LN2 = float(np.log(2.0))
AXES = ("x", "z", "y", "c")
SOURCE_AXES = ("x", "y")
TARGET_AXES = ("z", "c")
DIM = 32
DEPTH = 128
VEC = 3 * DIM
TILE = 512
CHUNK = 128
F32 = jnp.float32
BF16 = jnp.bfloat16
PARAMS = pltpu.CompilerParams(vmem_limit_bytes=48 << 20)


def split(v, count):
    pieces = []
    for _ in range(count):
        piece = v.astype(BF16)
        pieces.append(piece.astype(F32))
        v = v - pieces[-1]
    return pieces


def vector_rows(first, second, width):
    def rows(v):
        if v is None:
            return [jnp.ones((1, width), F32)] * 3
        return split(v, 3)

    zeros = jnp.zeros((10, width), F32)
    return jnp.concatenate(rows(first) + rows(second) + [zeros], axis=0).astype(BF16)


def combine(parts):
    top = jnp.max(parts, axis=0)
    return top + jnp.log2(jnp.sum(jnp.exp2(parts - top[None]), axis=0))


def lse_pass(lhs_ref, rhs_ref, write):
    for at in range(0, rhs_ref.shape[1], TILE):
        rhs = rhs_ref[:, at : at + TILE]
        top = total = None
        for row in range(0, lhs_ref.shape[0], CHUNK):
            terms = jnp.dot(lhs_ref[row : row + CHUNK, :], rhs, preferred_element_type=F32)
            terms = terms.reshape(CHUNK // 8, 8, TILE)
            newtop = jnp.max(terms, axis=0)
            if top is not None:
                newtop = jnp.maximum(top, newtop)
            added = jnp.sum(jnp.exp2(terms - newtop[None]), axis=0)
            total = added if top is None else total * jnp.exp2(top - newtop) + added
            top = newtop
        peak = jnp.max(top, axis=0, keepdims=True)
        total = jnp.sum(total * jnp.exp2(top - peak), axis=0, keepdims=True)
        write(at, peak + jnp.log2(total))


def write_copies(out_ref):
    def write(at, value):
        out_ref[:, :, at : at + TILE] = jnp.broadcast_to(value[None], (out_ref.shape[0], 1, TILE))

    return write


def pack_kernel(src_hbm, tgt_hbm, lb_hbm, g_hbm, spack, tpack, ssq, tsq, src, tgt, lb, g, sems):
    pairs = ((src_hbm, src), (tgt_hbm, tgt), (lb_hbm, lb), (g_hbm, g))
    copies = [pltpu.make_async_copy(a, b, sems.at[i]) for i, (a, b) in enumerate(pairs)]
    for copy in copies:
        copy.start()
    for copy in copies:
        copy.wait()
    s_t, t_t = src[...], tgt[...]
    s_norm = jnp.sum(s_t * s_t, axis=0, keepdims=True)
    t_norm = jnp.sum(t_t * t_t, axis=0, keepdims=True)
    ssq[...] = s_norm
    tsq[...] = t_norm
    s_t = s_t * ((2.0 / EPSILON) * LOG2E)
    packed = jnp.concatenate([s_t[: DIM // 2], s_t[DIM // 2 :]], axis=1)
    spack[...] = packed
    h = (lb[...] + (g[...] - t_norm) / EPSILON) * LOG2E
    weights = lb[...] * LOG2E
    half = t_t.shape[1] // 2
    rows = [t_t[:, :half], t_t[:, half:], h[:, :half], h[:, half:], weights[:, :half], weights[:, half:]]
    packed = jnp.concatenate(rows + [jnp.zeros((4, half), F32)], axis=0)
    tpack[...] = jnp.broadcast_to(packed[None], tpack.shape)


def first_kernel(group0, group2, group4, group6, tpg, la, out, akm, bkm, lb, brm, bh, packs):
    own = la.shape[1]
    half = DIM // 2
    me = lax.axis_index(TARGET_AXES)
    groups = (group0, group2, group4, group6)
    for p in range(packs.shape[0]):
        packs[p] = groups[p // 4][half * (p % 4) : half * (p % 4 + 1)]
    pieces = []
    for p in range(0, packs.shape[0], 2):
        a, b = packs[p ^ me], packs[(p + 1) ^ me]
        top = jnp.concatenate([a[:, :own], b[:, :own]], axis=1)
        low = jnp.concatenate([a[:, own:], b[:, own:]], axis=1)
        pieces.append(jnp.concatenate([top, low], axis=0))
    s = jnp.concatenate(pieces, axis=1)
    s1, s2 = (v.astype(BF16) for v in split(s, 2))
    width = s.shape[1]
    none = jnp.zeros((1, width), F32)
    akm[...] = jnp.concatenate([s1, s1, s2, vector_rows(none, None, width), jnp.zeros((16, width), BF16)], axis=0)
    weights = jnp.concatenate([la[...] * LOG2E, jnp.zeros_like(la[...])], axis=1)
    out[:, :, width:] = jnp.broadcast_to(weights[None], (out.shape[0], 1, 2 * own))
    width = 2 * tpg.shape[2]
    none = jnp.zeros((1, width), F32)
    zeros = jnp.zeros((16, width), BF16)
    for p in range(tpg.shape[0]):
        at = slice(width * p, width * (p + 1))
        wide = lambda row, count: jnp.concatenate([tpg[p, row : row + count], tpg[p, row + count : row + 2 * count]], axis=1)
        t1, t2 = (v.astype(BF16) for v in split(wide(0, DIM), 2))
        h = wide(2 * DIM, 1)
        lb[:, at] = wide(2 * DIM + 2, 1)
        bkm[:, at] = jnp.concatenate([t1, t2, t1, vector_rows(None, none, width), zeros], axis=0)
        bh[...] = jnp.concatenate([t1, t2, t1, vector_rows(None, h, width), zeros], axis=0)
        brm[at, :] = bh[...].T
    lse_pass(brm, akm, write_copies(out))


def first_column_kernel(parts, akm, bkm, out, la, arm, tmp):
    rows = la.shape[1]
    own = rows // parts.shape[0]
    for p in range(0, parts.shape[0], 2):
        la[:, own * p : own * (p + 2)] = jnp.concatenate(
            [parts[p, :, rows : rows + own], parts[p + 1, :, rows : rows + own]], axis=1
        )
    column_kernel(parts.at[:, :, :rows], la, akm, bkm, out, arm, tmp)


def column_kernel(parts, la, akm, bkm, out, arm, tmp):
    k = la[...] - combine(parts[...])
    tmp[...] = akm[...]
    tmp[VEC : VEC + 16, :] = vector_rows(k, None, k.shape[1])
    arm[...] = tmp[...].T
    lse_pass(arm, bkm, write_copies(out))


def row_kernel(parts, lb, akm, bkm, out, brm, tmp):
    h = lb[...] - combine(parts[...])
    tmp[...] = bkm[...]
    tmp[VEC : VEC + 16, :] = vector_rows(None, h, h.shape[1])
    brm[...] = tmp[...].T
    lse_pass(brm, akm, write_copies(out))


def last_column_kernel(parts, la, akm, bkm, ssq, out, f, arm, tmp):
    rows = combine(parts[...])
    me = lax.axis_index(TARGET_AXES)
    own = f.shape[1]
    mine = jnp.zeros((1, own), F32)
    for p in range(rows.shape[1] // own):
        mine = mine + jnp.where(me == p, rows[:, own * p : own * (p + 1)], 0.0)
    f[...] = ssq[...] - (EPSILON * LN2) * mine
    k = la[...] - rows
    tmp[...] = akm[...]
    tmp[VEC : VEC + 16, :] = vector_rows(k, None, k.shape[1])
    arm[...] = tmp[...].T

    def write(at, value):
        for own in range(0, TILE, out.shape[2]):
            out[(at + own) // out.shape[2]] = value[:, own : own + out.shape[2]]

    lse_pass(arm, bkm, write)


def last_kernel(parts, tsq, g):
    g[...] = tsq[...] - (EPSILON * LN2) * combine(parts[...])


def call(kernel, name, outs, *args, scratch=(), inputs=pltpu.VMEM):
    whole = pl.BlockSpec(memory_space=pltpu.VMEM)
    return pl.pallas_call(
        kernel,
        name=name,
        out_shape=[jax.ShapeDtypeStruct(*o) for o in outs],
        in_specs=[pl.BlockSpec(memory_space=inputs)] * len(args),
        out_specs=[whole] * len(outs),
        scratch_shapes=list(scratch),
        compiler_params=PARAMS,
    )(*args)


def exchange(v, axes):
    return lax.all_to_all(v, axes, 0, 0, tiled=True)


def swap(v, axis, offset):
    size = lax.axis_size(axis)
    return lax.ppermute(v, axis, [(i, i ^ offset) for i in range(size)])


def local(src_points, log_a, tgt_points, log_b, g_init):
    own_s, own_t = src_points.shape[0], tgt_points.shape[0]
    across_t = lax.axis_size(TARGET_AXES)
    across_s = lax.axis_size(SOURCE_AXES)
    rows, cols = own_s * across_t, own_t * across_s
    row = lambda v: v.reshape(1, -1)
    spack, tpack, ssq, tsq = call(
        pack_kernel,
        "pack",
        [
            ((DIM // 2, 2 * own_s), F32),
            ((across_s, 2 * DIM + 8, own_t // 2), F32),
            ((1, own_s), F32),
            ((1, own_t), F32),
        ],
        *(pltpu.with_memory_space_constraint(v, pltpu.HBM) for v in (src_points.T, tgt_points.T, row(log_b), row(g_init))),
        scratch=[pltpu.VMEM((DIM, own_s), F32), pltpu.VMEM((DIM, own_t), F32)]
        + [pltpu.VMEM((1, own_t), F32)] * 2
        + [pltpu.SemaphoreType.DMA((4,))],
        inputs=pltpu.HBM,
    )
    group = jnp.concatenate([spack, swap(spack, "c", 1)], axis=0)
    group = jnp.concatenate([group, swap(group, "z", 1)], axis=0)
    groups = [group] + [swap(group, "z", k) for k in (2, 4, 6)]
    tpg = exchange(tpack, SOURCE_AXES)
    row_out = ((across_t, 1, rows), F32)
    col_out = ((across_s, 1, cols), F32)
    parts, akm, bkm, lb = call(
        first_kernel,
        "row_pass_first",
        [((across_t, 1, rows + 2 * own_s), F32), ((DEPTH, rows), BF16), ((DEPTH, cols), BF16), ((1, cols), F32)],
        *groups,
        tpg,
        row(log_a),
        scratch=[pltpu.VMEM((cols, DEPTH), BF16), pltpu.VMEM((DEPTH, own_t), BF16)]
        + [pltpu.VMEM((across_t, DIM // 2, 2 * own_s), F32)],
    )
    row_scratch = [pltpu.VMEM((cols, DEPTH), BF16), pltpu.VMEM((DEPTH, cols), BF16)]
    col_scratch = [pltpu.VMEM((rows, DEPTH), BF16), pltpu.VMEM((DEPTH, rows), BF16)]
    parts = exchange(parts, TARGET_AXES)
    parts, la = call(
        first_column_kernel, "column_pass", [col_out, ((1, rows), F32)], parts, akm, bkm, scratch=col_scratch
    )
    parts = exchange(parts, SOURCE_AXES)
    (parts,) = call(row_kernel, "row_pass", [row_out], parts, lb, akm, bkm, scratch=row_scratch)
    parts = exchange(parts, TARGET_AXES)
    parts, f = call(
        last_column_kernel,
        "column_pass_last",
        [((across_s, 1, own_t), F32), ((1, own_s), F32)],
        parts,
        la,
        akm,
        bkm,
        ssq,
        scratch=col_scratch,
    )
    parts = exchange(parts, SOURCE_AXES)
    (g,) = call(last_kernel, "last", [((1, own_t), F32)], parts, tsq)
    return f.reshape(own_s), g.reshape(own_t)


def solution(mesh):
    fine = Mesh(mesh.devices.reshape(4, 8, 4, 2), AXES)
    flat = P(AXES)
    return jax.shard_map(
        local,
        mesh=fine,
        in_specs=(P(AXES, None), flat, P(AXES, None), flat, flat),
        out_specs=(flat, flat),
        check_vma=False,
    )
```

```python
import functools

import jax
import jax.numpy as jnp
import numpy as np
from jax import lax
from jax.experimental import pallas as pl
from jax.experimental.pallas import tpu as pltpu
from jax.sharding import Mesh
from jax.sharding import PartitionSpec as P

EPSILON = 0.5
LOG2E = float(np.log2(np.e))
LN2 = float(np.log(2.0))
AXES = ("x", "z", "y", "c")
SOURCE_AXES = ("x", "y")
TARGET_AXES = ("z", "c")
DIM = 32
DEPTH = 128
VEC = 3 * DIM
TILE = 256
CHUNK = 128
OVERFLOW = 1e38
F32 = jnp.float32
BF16 = jnp.bfloat16
JOIN_COST = pl.CostEstimate(flops=1000000000000, bytes_accessed=0, transcendentals=0)


def split(v, count):
    pieces = []
    for _ in range(count):
        piece = v.astype(BF16)
        pieces.append(piece.astype(F32))
        v = v - pieces[-1]
    return pieces


def vector_rows(first, second, width):
    def rows(v):
        if v is None:
            return [jnp.ones((1, width), F32)] * 3
        return split(v, 3)

    zeros = jnp.zeros((10, width), F32)
    return jnp.concatenate(rows(first) + rows(second) + [zeros], axis=0).astype(BF16)


def combine(parts):
    top = jnp.max(parts, axis=0)
    return top + jnp.log2(jnp.sum(jnp.exp2(parts - top[None]), axis=0))


def lse_pass(lhs_ref, rhs_ref, write):
    largest = None
    for at in range(0, rhs_ref.shape[1], TILE):
        rhs = rhs_ref[:, at : at + TILE]
        top = total = None
        for row in range(0, lhs_ref.shape[0], CHUNK):
            terms = jnp.dot(lhs_ref[row : row + CHUNK, :], rhs, preferred_element_type=F32)
            terms = terms.reshape(CHUNK // 8, 8, TILE)
            if top is None:
                top = jnp.max(jnp.max(terms, axis=0), axis=0, keepdims=True)
            added = jnp.sum(jnp.exp2(terms - top[None]), axis=0)
            total = added if total is None else total + added
        total = jnp.sum(total, axis=0, keepdims=True)
        largest = total if largest is None else jnp.maximum(largest, total)
        write(at // TILE, top + jnp.log2(total))

    @pl.when(jnp.logical_not(jnp.max(largest) < OVERFLOW))
    def _():
        running_lse_pass(lhs_ref, rhs_ref, write)


def running_lse_pass(lhs_ref, rhs_ref, write):
    def tile(n, carry):
        rhs = rhs_ref[:, pl.ds(pl.multiple_of(n * TILE, TILE), TILE)]

        def step(r, state):
            top, total = state
            lhs = lhs_ref[pl.ds(pl.multiple_of(r * CHUNK, CHUNK), CHUNK), :]
            terms = jnp.dot(lhs, rhs, preferred_element_type=F32).reshape(CHUNK // 8, 8, TILE)
            newtop = jnp.maximum(top, jnp.max(terms, axis=0))
            added = jnp.sum(jnp.exp2(terms - newtop[None]), axis=0)
            return newtop, total * jnp.exp2(top - newtop) + added

        start = (jnp.full((8, TILE), -1e30, F32), jnp.zeros((8, TILE), F32))
        top, total = lax.fori_loop(0, lhs_ref.shape[0] // CHUNK, step, start, unroll=8)
        peak = jnp.max(top, axis=0, keepdims=True)
        total = jnp.sum(total * jnp.exp2(top - peak), axis=0, keepdims=True)
        write(n, peak + jnp.log2(total))
        return carry

    lax.fori_loop(0, rhs_ref.shape[1] // TILE, tile, 0)


def write_copies(out_ref):
    def write(n, value):
        at = pl.ds(n * TILE if isinstance(n, int) else pl.multiple_of(n * TILE, TILE), TILE)
        out_ref[:, :, at] = jnp.broadcast_to(value[None], (out_ref.shape[0], 1, TILE))

    return write


def pack_kernel(src_hbm, tgt_hbm, lb_hbm, g_hbm, spack, tpack, ssq, tsq, src, tgt, lb, g, sems):
    pairs = ((src_hbm, src), (tgt_hbm, tgt), (lb_hbm, lb), (g_hbm, g))
    copies = [pltpu.make_async_copy(a, b, sems.at[i]) for i, (a, b) in enumerate(pairs)]
    for copy in copies:
        copy.start()
    for copy in copies:
        copy.wait()
    s_t, t_t = src[...], tgt[...]
    s_norm = jnp.sum(s_t * s_t, axis=0, keepdims=True)
    t_norm = jnp.sum(t_t * t_t, axis=0, keepdims=True)
    ssq[...] = s_norm
    tsq[...] = t_norm
    s_t = s_t * ((2.0 / EPSILON) * LOG2E)
    packed = jnp.concatenate([s_t[: DIM // 2], s_t[DIM // 2 :]], axis=1)
    spack[...] = packed
    h = (lb[...] + (g[...] - t_norm) / EPSILON) * LOG2E
    weights = lb[...] * LOG2E
    half = t_t.shape[1] // 2
    rows = [t_t[:, :half], t_t[:, half:], h[:, :half], h[:, half:], weights[:, :half], weights[:, half:]]
    packed = jnp.concatenate(rows + [jnp.zeros((4, half), F32)], axis=0)
    tpack[...] = jnp.broadcast_to(packed[None], tpack.shape)


def join_kernel(first, second, out):
    rows = first.shape[0]
    out[:rows] = first[...]
    out[rows:] = second[...]


def first_kernel(even, odd, even_c, odd_c, tpg, la, out, akm, bkm, lb, brm, bh, packs):
    own = la.shape[1]
    half = DIM // 2
    me = lax.axis_index(TARGET_AXES)
    for at, offset in enumerate((0, 4, 2, 6)):
        row = slice(half * at, half * (at + 1))
        for other, group in enumerate((even, even_c, odd, odd_c)):
            packs[2 * offset + other] = group[row]
    pieces = []
    for p in range(0, packs.shape[0], 2):
        a, b = packs[p ^ me], packs[(p + 1) ^ me]
        top = jnp.concatenate([a[:, :own], b[:, :own]], axis=1)
        low = jnp.concatenate([a[:, own:], b[:, own:]], axis=1)
        pieces.append(jnp.concatenate([top, low], axis=0))
    s = jnp.concatenate(pieces, axis=1)
    s1, s2 = (v.astype(BF16) for v in split(s, 2))
    width = s.shape[1]
    none = jnp.zeros((1, width), F32)
    akm[...] = jnp.concatenate([s1, s1, s2, vector_rows(none, None, width), jnp.zeros((16, width), BF16)], axis=0)
    weights = jnp.concatenate([la[...] * LOG2E, jnp.zeros_like(la[...])], axis=1)
    out[:, :, width:] = jnp.broadcast_to(weights[None], (out.shape[0], 1, 2 * own))
    width = 2 * tpg.shape[2]
    none = jnp.zeros((1, width), F32)
    zeros = jnp.zeros((16, width), BF16)
    for p in range(tpg.shape[0]):
        at = slice(width * p, width * (p + 1))
        wide = lambda row, count: jnp.concatenate([tpg[p, row : row + count], tpg[p, row + count : row + 2 * count]], axis=1)
        t1, t2 = (v.astype(BF16) for v in split(wide(0, DIM), 2))
        h = wide(2 * DIM, 1)
        lb[:, at] = wide(2 * DIM + 2, 1)
        bkm[:, at] = jnp.concatenate([t1, t2, t1, vector_rows(None, none, width), zeros], axis=0)
        bh[...] = jnp.concatenate([t1, t2, t1, vector_rows(None, h, width), zeros], axis=0)
        brm[at, :] = bh[...].T
    lse_pass(brm, akm, write_copies(out))


def first_column_kernel(parts, akm, bkm, out, la, arm, tmp):
    rows = la.shape[1]
    own = rows // parts.shape[0]
    for p in range(0, parts.shape[0], 2):
        la[:, own * p : own * (p + 2)] = jnp.concatenate(
            [parts[p, :, rows : rows + own], parts[p + 1, :, rows : rows + own]], axis=1
        )
    column_kernel(parts.at[:, :, :rows], la, akm, bkm, out, arm, tmp)


def column_kernel(parts, la, akm, bkm, out, arm, tmp):
    k = la[...] - combine(parts[...])
    tmp[...] = akm[...]
    tmp[VEC : VEC + 16, :] = vector_rows(k, None, k.shape[1])
    arm[...] = tmp[...].T
    lse_pass(arm, bkm, write_copies(out))


def row_kernel(parts, lb, akm, bkm, out, brm, tmp):
    h = lb[...] - combine(parts[...])
    tmp[...] = bkm[...]
    tmp[VEC : VEC + 16, :] = vector_rows(None, h, h.shape[1])
    brm[...] = tmp[...].T
    lse_pass(brm, akm, write_copies(out))


def last_column_kernel(parts, la, akm, bkm, ssq, out, f, arm, tmp):
    rows = combine(parts[...])
    me = lax.axis_index(TARGET_AXES)
    own = f.shape[1]
    mine = jnp.zeros((1, own), F32)
    for p in range(rows.shape[1] // own):
        mine = mine + jnp.where(me == p, rows[:, own * p : own * (p + 1)], 0.0)
    f[...] = ssq[...] - (EPSILON * LN2) * mine
    k = la[...] - rows
    tmp[...] = akm[...]
    tmp[VEC : VEC + 16, :] = vector_rows(k, None, k.shape[1])
    arm[...] = tmp[...].T

    def write(n, value):
        out[n] = value

    lse_pass(arm, bkm, write)


def last_kernel(parts, tsq, g):
    g[...] = tsq[...] - (EPSILON * LN2) * combine(parts[...])


def call(kernel, name, outs, *args, scratch=(), inputs=pltpu.VMEM, cost=None, vmem=48):
    whole = pl.BlockSpec(memory_space=pltpu.VMEM)
    return pl.pallas_call(
        kernel,
        name=name,
        out_shape=[jax.ShapeDtypeStruct(*o) for o in outs],
        in_specs=[pl.BlockSpec(memory_space=inputs)] * len(args),
        out_specs=[whole] * len(outs),
        scratch_shapes=list(scratch),
        compiler_params=pltpu.CompilerParams(vmem_limit_bytes=vmem << 20),
        cost_estimate=cost,
    )(*args)


def exchange(v, axes):
    return lax.all_to_all(v, axes, 0, 0, tiled=True)


def swap(v, axis, offset):
    size = lax.axis_size(axis)
    return lax.ppermute(v, axis, [(i, i ^ offset) for i in range(size)])


def local(src_points, log_a, tgt_points, log_b, g_init):
    own_s, own_t = src_points.shape[0], tgt_points.shape[0]
    across_t = lax.axis_size(TARGET_AXES)
    across_s = lax.axis_size(SOURCE_AXES)
    rows, cols = own_s * across_t, own_t * across_s
    row = lambda v: v.reshape(1, -1)
    spack, tpack, ssq, tsq = call(
        pack_kernel,
        "pack",
        [
            ((DIM // 2, 2 * own_s), F32),
            ((across_s, 2 * DIM + 8, own_t // 2), F32),
            ((1, own_s), F32),
            ((1, own_t), F32),
        ],
        *(pltpu.with_memory_space_constraint(v, pltpu.HBM) for v in (src_points.T, tgt_points.T, row(log_b), row(g_init))),
        scratch=[pltpu.VMEM((DIM, own_s), F32), pltpu.VMEM((DIM, own_t), F32)]
        + [pltpu.VMEM((1, own_t), F32)] * 2
        + [pltpu.SemaphoreType.DMA((4,))],
        inputs=pltpu.HBM,
        vmem=8,
    )
    pair = call(
        join_kernel, "join", [((DIM, 2 * own_s), F32)], spack, swap(spack, "z", 4), cost=JOIN_COST, vmem=2
    )[0]
    even = jnp.concatenate([pair, swap(pair, "z", 2)], axis=0)
    odd = swap(even, "z", 1)
    groups = [even, odd, swap(even, "c", 1), swap(odd, "c", 1)]
    tpg = exchange(tpack, SOURCE_AXES)
    row_out = ((across_t, 1, rows), F32)
    col_out = ((across_s, 1, cols), F32)
    parts, akm, bkm, lb = call(
        first_kernel,
        "row_pass_first",
        [((across_t, 1, rows + 2 * own_s), F32), ((DEPTH, rows), BF16), ((DEPTH, cols), BF16), ((1, cols), F32)],
        *groups,
        tpg,
        row(log_a),
        scratch=[pltpu.VMEM((cols, DEPTH), BF16), pltpu.VMEM((DEPTH, own_t), BF16)]
        + [pltpu.VMEM((across_t, DIM // 2, 2 * own_s), F32)],
    )
    row_scratch = [pltpu.VMEM((cols, DEPTH), BF16), pltpu.VMEM((DEPTH, cols), BF16)]
    col_scratch = [pltpu.VMEM((rows, DEPTH), BF16), pltpu.VMEM((DEPTH, rows), BF16)]
    parts = exchange(parts, TARGET_AXES)
    parts, la = call(
        first_column_kernel, "column_pass", [col_out, ((1, rows), F32)], parts, akm, bkm, scratch=col_scratch
    )
    parts = exchange(parts, SOURCE_AXES)
    (parts,) = call(row_kernel, "row_pass", [row_out], parts, lb, akm, bkm, scratch=row_scratch)
    parts = exchange(parts, TARGET_AXES)
    parts, f = call(
        last_column_kernel,
        "column_pass_last",
        [((across_s, 1, own_t), F32), ((1, own_s), F32)],
        parts,
        la,
        akm,
        bkm,
        ssq,
        scratch=col_scratch,
    )
    parts = exchange(parts, SOURCE_AXES)
    (g,) = call(last_kernel, "last", [((1, own_t), F32)], parts, tsq)
    return f.reshape(own_s), g.reshape(own_t)


def solution(mesh):
    fine = Mesh(mesh.devices.reshape(4, 8, 4, 2), AXES)
    flat = P(AXES)
    return jax.shard_map(
        local,
        mesh=fine,
        in_specs=(P(AXES, None), flat, P(AXES, None), flat, flat),
        out_specs=(flat, flat),
        check_vma=False,
    )
```

```python
import jax
import jax.numpy as jnp
import numpy as np
from jax import lax
from jax.experimental import pallas as pl
from jax.experimental.pallas import tpu as pltpu
from jax.sharding import Mesh
from jax.sharding import PartitionSpec as P

EPSILON = 0.5
LOG2E = float(np.log2(np.e))
LN2 = float(np.log(2.0))
AXES = ("x", "z", "y", "c")
SOURCE_AXES = ("x", "y")
TARGET_AXES = ("z", "c")
DIM = 32
DEPTH = 128
VEC = 3 * DIM
TILE = 256
CHUNK = 128
OVERFLOW = 1e38
F32 = jnp.float32
BF16 = jnp.bfloat16
Z_ORDER = (0, 4, 1, 5, 2, 6, 3, 7)
JOIN_COST = pl.CostEstimate(flops=1000000000000, bytes_accessed=0, transcendentals=0)


def split(v, count):
    pieces = []
    for _ in range(count):
        piece = v.astype(BF16)
        pieces.append(piece.astype(F32))
        v = v - pieces[-1]
    return pieces


def vector_rows(first, second, width):
    def rows(v):
        if v is None:
            return [jnp.ones((1, width), F32)] * 3
        return split(v, 3)

    zeros = jnp.zeros((10, width), F32)
    return jnp.concatenate(rows(first) + rows(second) + [zeros], axis=0).astype(BF16)


def combine(parts):
    top = jnp.max(parts, axis=0)
    return top + jnp.log2(jnp.sum(jnp.exp2(parts - top[None]), axis=0))


def lse_pass(lhs_t, lhs_ref, rhs_ref, write):
    largest = None
    for at in range(0, rhs_ref.shape[1], TILE):
        rhs = rhs_ref[:, at : at + TILE]
        top = total = None
        for row in range(0, lhs_ref.shape[0], CHUNK):
            if at == 0:
                lhs = lhs_t[:, row : row + CHUNK].T
                lhs_ref[row : row + CHUNK, :] = lhs
            else:
                lhs = lhs_ref[row : row + CHUNK, :]
            terms = jnp.dot(lhs, rhs, preferred_element_type=F32).reshape(CHUNK // 8, 8, TILE)
            if top is None:
                top = jnp.max(jnp.max(terms, axis=0), axis=0, keepdims=True)
            added = jnp.sum(jnp.exp2(terms - top[None]), axis=0)
            total = added if total is None else total + added
        total = jnp.sum(total, axis=0, keepdims=True)
        largest = total if largest is None else jnp.maximum(largest, total)
        write(at // TILE, top + jnp.log2(total))

    @pl.when(jnp.logical_not(jnp.max(largest) < OVERFLOW))
    def _():
        running_lse_pass(lhs_ref, rhs_ref, write)


def running_lse_pass(lhs_ref, rhs_ref, write):
    def tile(n, carry):
        rhs = rhs_ref[:, pl.ds(pl.multiple_of(n * TILE, TILE), TILE)]

        def step(r, state):
            top, total = state
            lhs = lhs_ref[pl.ds(pl.multiple_of(r * CHUNK, CHUNK), CHUNK), :]
            terms = jnp.dot(lhs, rhs, preferred_element_type=F32).reshape(CHUNK // 8, 8, TILE)
            newtop = jnp.maximum(top, jnp.max(terms, axis=0))
            added = jnp.sum(jnp.exp2(terms - newtop[None]), axis=0)
            return newtop, total * jnp.exp2(top - newtop) + added

        start = (jnp.full((8, TILE), -1e30, F32), jnp.zeros((8, TILE), F32))
        top, total = lax.fori_loop(0, lhs_ref.shape[0] // CHUNK, step, start, unroll=8)
        peak = jnp.max(top, axis=0, keepdims=True)
        total = jnp.sum(total * jnp.exp2(top - peak), axis=0, keepdims=True)
        write(n, peak + jnp.log2(total))
        return carry

    lax.fori_loop(0, rhs_ref.shape[1] // TILE, tile, 0)


def write_dense(out_ref):
    per_row = out_ref.shape[2] // TILE

    def write(n, value):
        at = pl.ds(n % per_row * TILE if isinstance(n, int) else pl.multiple_of(n % per_row * TILE, TILE), TILE)
        out_ref[:, pl.ds(n // per_row, 1), at] = jnp.broadcast_to(value[None], (out_ref.shape[0], 1, TILE))

    return write


def write_copies(out_ref):
    def write(n, value):
        at = pl.ds(n * TILE if isinstance(n, int) else pl.multiple_of(n * TILE, TILE), TILE)
        out_ref[:, :, at] = jnp.broadcast_to(value[None], (out_ref.shape[0], 1, TILE))

    return write


def pack_kernel(src_hbm, tgt_hbm, lb_hbm, g_hbm, spack, tpack, ssq, tsq, src, tgt, lb, g, sems):
    pairs = ((src_hbm, src), (tgt_hbm, tgt), (lb_hbm, lb), (g_hbm, g))
    copies = [pltpu.make_async_copy(a, b, sems.at[i]) for i, (a, b) in enumerate(pairs)]
    for copy in copies:
        copy.start()
    for copy in copies:
        copy.wait()
    s_t, t_t = src[...], tgt[...]
    s_norm = jnp.sum(s_t * s_t, axis=0, keepdims=True)
    t_norm = jnp.sum(t_t * t_t, axis=0, keepdims=True)
    ssq[...] = s_norm
    tsq[...] = t_norm
    s_t = s_t * ((2.0 / EPSILON) * LOG2E)
    packed = jnp.concatenate([s_t[: DIM // 2], s_t[DIM // 2 :]], axis=1)
    spack[...] = packed
    h = (lb[...] + (g[...] - t_norm) / EPSILON) * LOG2E
    weights = lb[...] * LOG2E
    half = t_t.shape[1] // 2
    rows = [t_t[:, :half], t_t[:, half:], h[:, :half], h[:, half:], weights[:, :half], weights[:, half:]]
    packed = jnp.concatenate(rows + [jnp.zeros((4, half), F32)], axis=0)
    tpack[...] = jnp.broadcast_to(packed[None], tpack.shape)


def join_kernel(first, second, out):
    rows = first.shape[0]
    out[:rows] = first[...]
    out[rows:] = second[...]


def first_kernel(mine, other, tpg_hbm, la_hbm, out, akm, bkm, lb, brm, bh, packs, tpg, la, sems):
    copies = [pltpu.make_async_copy(la_hbm, la, sems.at[0])]
    for p in range(tpg.shape[0]):
        copies.append(pltpu.make_async_copy(tpg_hbm.at[p], tpg.at[p], sems.at[p + 1]))
    for copy in copies:
        copy.start()
    own = la.shape[1]
    half = DIM // 2
    me = lax.axis_index(TARGET_AXES)
    for at, offset in enumerate(Z_ORDER):
        row = slice(half * at, half * (at + 1))
        packs[2 * offset], packs[2 * offset + 1] = mine[row], other[row]
    pieces = []
    for p in range(0, packs.shape[0], 2):
        a, b = packs[p ^ me], packs[(p + 1) ^ me]
        top = jnp.concatenate([a[:, :own], b[:, :own]], axis=1)
        low = jnp.concatenate([a[:, own:], b[:, own:]], axis=1)
        pieces.append(jnp.concatenate([top, low], axis=0))
    s = jnp.concatenate(pieces, axis=1)
    s1, s2 = (v.astype(BF16) for v in split(s, 2))
    width = s.shape[1]
    none = jnp.zeros((1, width), F32)
    akm[...] = jnp.concatenate([s1, s1, s2, vector_rows(none, None, width), jnp.zeros((16, width), BF16)], axis=0)
    copies[0].wait()
    weights = jnp.concatenate([la[...] * LOG2E, jnp.zeros_like(la[...])], axis=1)
    out[:, :, width:] = jnp.broadcast_to(weights[None], (out.shape[0], 1, 2 * own))
    width = 2 * tpg.shape[2]
    none = jnp.zeros((1, width), F32)
    zeros = jnp.zeros((16, width), BF16)
    for p in range(tpg.shape[0]):
        copies[p + 1].wait()
        at = slice(width * p, width * (p + 1))
        wide = lambda row, count: jnp.concatenate([tpg[p, row : row + count], tpg[p, row + count : row + 2 * count]], axis=1)
        t1, t2 = (v.astype(BF16) for v in split(wide(0, DIM), 2))
        h = wide(2 * DIM, 1)
        lb[:, at] = wide(2 * DIM + 2, 1)
        bkm[:, at] = jnp.concatenate([t1, t2, t1, vector_rows(None, none, width), zeros], axis=0)
        bh[:, at] = jnp.concatenate([t1, t2, t1, vector_rows(None, h, width), zeros], axis=0)
    lse_pass(bh, brm, akm, write_copies(out))


def first_column_kernel(parts, akm, bkm, out, la, arm, tmp):
    rows = la.shape[1]
    own = rows // parts.shape[0]
    for p in range(0, parts.shape[0], 2):
        la[:, own * p : own * (p + 2)] = jnp.concatenate(
            [parts[p, :, rows : rows + own], parts[p + 1, :, rows : rows + own]], axis=1
        )
    k = la[...] - combine(parts[:, :, :rows])
    tmp[...] = akm[...]
    tmp[VEC : VEC + 16, :] = vector_rows(k, None, k.shape[1])
    lse_pass(tmp, arm, bkm, write_dense(out))


def row_kernel(parts, lb, akm, bkm, out, brm, tmp):
    dense = combine(parts[...])
    h = lb[...] - jnp.concatenate([dense[r : r + 1] for r in range(dense.shape[0])], axis=1)
    tmp[...] = bkm[...]
    tmp[VEC : VEC + 16, :] = vector_rows(None, h, h.shape[1])
    lse_pass(tmp, brm, akm, write_copies(out))


def last_column_kernel(parts, la, akm, bkm, out, own_rows, arm, tmp):
    rows = combine(parts[...])
    me = lax.axis_index(TARGET_AXES)
    own = own_rows.shape[1]
    mine = jnp.zeros((1, own), F32)
    for p in range(rows.shape[1] // own):
        mine = mine + jnp.where(me == p, rows[:, own * p : own * (p + 1)], 0.0)
    own_rows[...] = mine
    k = la[...] - rows
    tmp[...] = akm[...]
    tmp[VEC : VEC + 16, :] = vector_rows(k, None, k.shape[1])

    def write(n, value):
        out[n] = value

    lse_pass(tmp, arm, bkm, write)


def last_kernel(parts, own_rows, ssq, tsq, f, g):
    f[...] = ssq[...] - (EPSILON * LN2) * own_rows[...]
    g[...] = tsq[...] - (EPSILON * LN2) * combine(parts[...])


def call(kernel, name, outs, *args, scratch=(), inputs=None, cost=None, vmem=48):
    whole = pl.BlockSpec(memory_space=pltpu.VMEM)
    return pl.pallas_call(
        kernel,
        name=name,
        out_shape=[jax.ShapeDtypeStruct(*o) for o in outs],
        in_specs=[pl.BlockSpec(memory_space=space) for space in inputs or [pltpu.VMEM] * len(args)],
        out_specs=[whole] * len(outs),
        scratch_shapes=list(scratch),
        compiler_params=pltpu.CompilerParams(vmem_limit_bytes=vmem << 20),
        cost_estimate=cost,
    )(*args)


def exchange(v, axes):
    return lax.all_to_all(v, axes, 0, 0, tiled=True)


def swap(v, axis, offset):
    size = lax.axis_size(axis)
    return lax.ppermute(v, axis, [(i, i ^ offset) for i in range(size)])


def pinned(*arrays):
    return [pltpu.with_memory_space_constraint(v, pltpu.HBM) for v in arrays]


def local(src_points, log_a, tgt_points, log_b, g_init):
    own_s, own_t = src_points.shape[0], tgt_points.shape[0]
    across_t = lax.axis_size(TARGET_AXES)
    across_s = lax.axis_size(SOURCE_AXES)
    rows, cols = own_s * across_t, own_t * across_s
    row = lambda v: v.reshape(1, -1)
    spack, tpack, ssq, tsq = call(
        pack_kernel,
        "pack",
        [
            ((DIM // 2, 2 * own_s), F32),
            ((across_s, 2 * DIM + 8, own_t // 2), F32),
            ((1, own_s), F32),
            ((1, own_t), F32),
        ],
        *pinned(src_points.T, tgt_points.T, row(log_b), row(g_init)),
        scratch=[pltpu.VMEM((DIM, own_s), F32), pltpu.VMEM((DIM, own_t), F32)]
        + [pltpu.VMEM((1, own_t), F32)] * 2
        + [pltpu.SemaphoreType.DMA((4,))],
        inputs=[pltpu.HBM] * 4,
        vmem=8,
    )
    pair = call(
        join_kernel, "join", [((DIM, 2 * own_s), F32)], spack, swap(spack, "z", 4), cost=JOIN_COST, vmem=2
    )[0]
    mine = jnp.concatenate([pair] + [swap(pair, "z", k) for k in (1, 2, 3)], axis=0)
    groups = [mine, swap(mine, "c", 1)]
    tpg = exchange(tpack, SOURCE_AXES)
    row_out = ((across_t, 1, rows), F32)
    col_out = ((across_s, 8, cols // 8), F32)
    parts, akm, bkm, lb = call(
        first_kernel,
        "row_pass_first",
        [((across_t, 1, rows + 2 * own_s), F32), ((DEPTH, rows), BF16), ((DEPTH, cols), BF16), ((1, cols), F32)],
        *groups,
        *pinned(tpg, row(log_a)),
        scratch=[pltpu.VMEM((cols, DEPTH), BF16), pltpu.VMEM((DEPTH, cols), BF16)]
        + [pltpu.VMEM((across_t, DIM // 2, 2 * own_s), F32), pltpu.VMEM(tpg.shape, F32)]
        + [pltpu.VMEM((1, own_s), F32), pltpu.SemaphoreType.DMA((across_s + 1,))],
        inputs=[pltpu.VMEM] * 2 + [pltpu.HBM] * 2,
    )
    row_scratch = [pltpu.VMEM((cols, DEPTH), BF16), pltpu.VMEM((DEPTH, cols), BF16)]
    col_scratch = [pltpu.VMEM((rows, DEPTH), BF16), pltpu.VMEM((DEPTH, rows), BF16)]
    parts = exchange(parts, TARGET_AXES)
    parts, la = call(
        first_column_kernel, "column_pass", [col_out, ((1, rows), F32)], parts, akm, bkm, scratch=col_scratch
    )
    parts = exchange(parts, SOURCE_AXES)
    (parts,) = call(row_kernel, "row_pass", [row_out], parts, lb, akm, bkm, scratch=row_scratch)
    parts = exchange(parts, TARGET_AXES)
    parts, own_rows = call(
        last_column_kernel,
        "column_pass_last",
        [((across_s, 1, own_t), F32), ((1, own_s), F32)],
        parts,
        la,
        akm,
        bkm,
        scratch=col_scratch,
    )
    parts = exchange(parts, SOURCE_AXES)
    f, g = call(last_kernel, "last", [((1, own_s), F32), ((1, own_t), F32)], parts, own_rows, ssq, tsq)
    return f.reshape(own_s), g.reshape(own_t)


def solution(mesh):
    fine = Mesh(mesh.devices.reshape(4, 8, 4, 2), AXES)
    flat = P(AXES)
    return jax.shard_map(
        local,
        mesh=fine,
        in_specs=(P(AXES, None), flat, P(AXES, None), flat, flat),
        out_specs=(flat, flat),
        check_vma=False,
    )
```

```python
import jax
import jax.numpy as jnp
import numpy as np
from jax import lax
from jax.experimental import pallas as pl
from jax.experimental.pallas import tpu as pltpu
from jax.sharding import Mesh
from jax.sharding import PartitionSpec as P

EPSILON = 0.5
LOG2E = float(np.log2(np.e))
LN2 = float(np.log(2.0))
AXES = ("x", "z", "y", "c")
SOURCE_AXES = ("y", "x")
TARGET_AXES = ("c", "z")
DIM = 32
DEPTH = 128
VEC = 3 * DIM
TILE = 256
CHUNK = 128
OVERFLOW = 1e38
F32 = jnp.float32
BF16 = jnp.bfloat16
Z_ORDER = (0, 4, 1, 5, 2, 6, 3, 7)
JOIN_COST = pl.CostEstimate(flops=1000000000000, bytes_accessed=0, transcendentals=0)


def split(v, count):
    pieces = []
    for _ in range(count):
        piece = v.astype(BF16)
        pieces.append(piece.astype(F32))
        v = v - pieces[-1]
    return pieces


def vector_rows(first, second, width):
    def rows(v):
        if v is None:
            return [jnp.ones((1, width), F32)] * 3
        return split(v, 3)

    zeros = jnp.zeros((10, width), F32)
    return jnp.concatenate(rows(first) + rows(second) + [zeros], axis=0).astype(BF16)


def combine(parts):
    top = jnp.max(parts, axis=0)
    return top + jnp.log2(jnp.sum(jnp.exp2(parts - top[None]), axis=0))


def lse_pass(lhs_t, lhs_ref, rhs_ref, write):
    largest = None
    for at in range(0, rhs_ref.shape[1], TILE):
        rhs = rhs_ref[:, at : at + TILE]
        top = total = None
        for row in range(0, lhs_ref.shape[0], CHUNK):
            if at == 0:
                lhs = lhs_t[:, row : row + CHUNK].T
                lhs_ref[row : row + CHUNK, :] = lhs
            else:
                lhs = lhs_ref[row : row + CHUNK, :]
            terms = jnp.dot(lhs, rhs, preferred_element_type=F32).reshape(CHUNK // 8, 8, TILE)
            if top is None:
                top = jnp.max(jnp.max(terms, axis=0), axis=0, keepdims=True)
            added = jnp.sum(jnp.exp2(terms - top[None]), axis=0)
            total = added if total is None else total + added
        total = jnp.sum(total, axis=0, keepdims=True)
        largest = total if largest is None else jnp.maximum(largest, total)
        write(at // TILE, top + jnp.log2(total))

    @pl.when(jnp.logical_not(jnp.max(largest) < OVERFLOW))
    def _():
        running_lse_pass(lhs_ref, rhs_ref, write)


def running_lse_pass(lhs_ref, rhs_ref, write):
    def tile(n, carry):
        rhs = rhs_ref[:, pl.ds(pl.multiple_of(n * TILE, TILE), TILE)]

        def step(r, state):
            top, total = state
            lhs = lhs_ref[pl.ds(pl.multiple_of(r * CHUNK, CHUNK), CHUNK), :]
            terms = jnp.dot(lhs, rhs, preferred_element_type=F32).reshape(CHUNK // 8, 8, TILE)
            newtop = jnp.maximum(top, jnp.max(terms, axis=0))
            added = jnp.sum(jnp.exp2(terms - newtop[None]), axis=0)
            return newtop, total * jnp.exp2(top - newtop) + added

        start = (jnp.full((8, TILE), -1e30, F32), jnp.zeros((8, TILE), F32))
        top, total = lax.fori_loop(0, lhs_ref.shape[0] // CHUNK, step, start, unroll=8)
        peak = jnp.max(top, axis=0, keepdims=True)
        total = jnp.sum(total * jnp.exp2(top - peak), axis=0, keepdims=True)
        write(n, peak + jnp.log2(total))
        return carry

    lax.fori_loop(0, rhs_ref.shape[1] // TILE, tile, 0)


def write_dense(out_ref):
    per_row = out_ref.shape[2] // TILE

    def write(n, value):
        at = pl.ds(n % per_row * TILE if isinstance(n, int) else pl.multiple_of(n % per_row * TILE, TILE), TILE)
        out_ref[:, pl.ds(n // per_row, 1), at] = jnp.broadcast_to(value[None], (out_ref.shape[0], 1, TILE))

    return write


def write_copies(out_ref):
    def write(n, value):
        at = pl.ds(n * TILE if isinstance(n, int) else pl.multiple_of(n * TILE, TILE), TILE)
        out_ref[:, :, at] = jnp.broadcast_to(value[None], (out_ref.shape[0], 1, TILE))

    return write


def pack_kernel(src_hbm, tgt_hbm, lb_hbm, g_hbm, spack, tpack, ssq, tsq, src, tgt, lb, g, sems):
    pairs = ((src_hbm, src), (tgt_hbm, tgt), (lb_hbm, lb), (g_hbm, g))
    copies = [pltpu.make_async_copy(a, b, sems.at[i]) for i, (a, b) in enumerate(pairs)]
    for copy in copies:
        copy.start()
    for copy in copies:
        copy.wait()
    s_t, t_t = src[...], tgt[...]
    s_norm = jnp.sum(s_t * s_t, axis=0, keepdims=True)
    t_norm = jnp.sum(t_t * t_t, axis=0, keepdims=True)
    ssq[...] = s_norm
    tsq[...] = t_norm
    s_t = s_t * ((2.0 / EPSILON) * LOG2E)
    packed = jnp.concatenate([s_t[: DIM // 2], s_t[DIM // 2 :]], axis=1)
    spack[...] = packed
    h = (lb[...] + (g[...] - t_norm) / EPSILON) * LOG2E
    weights = lb[...] * LOG2E
    half = t_t.shape[1] // 2
    rows = [t_t[:, :half], t_t[:, half:], h[:, :half], h[:, half:], weights[:, :half], weights[:, half:]]
    packed = jnp.concatenate(rows + [jnp.zeros((4, half), F32)], axis=0)
    tpack[...] = jnp.broadcast_to(packed[None], tpack.shape)


def join_kernel(first, second, out):
    rows = first.shape[0]
    out[:rows] = first[...]
    out[rows:] = second[...]


def first_kernel(mine, other, tpg_hbm, la_hbm, out, akm, bkm, lb, brm, bh, packs, tpg, la, sems):
    copies = [pltpu.make_async_copy(la_hbm, la, sems.at[0])]
    for p in range(tpg.shape[0]):
        copies.append(pltpu.make_async_copy(tpg_hbm.at[p], tpg.at[p], sems.at[p + 1]))
    for copy in copies:
        copy.start()
    own = la.shape[1]
    half = DIM // 2
    me = lax.axis_index(TARGET_AXES)
    for at, offset in enumerate(Z_ORDER):
        row = slice(half * at, half * (at + 1))
        packs[offset], packs[offset + 8] = mine[row], other[row]
    pieces = []
    for p in range(0, packs.shape[0], 2):
        a, b = packs[p ^ me], packs[(p + 1) ^ me]
        top = jnp.concatenate([a[:, :own], b[:, :own]], axis=1)
        low = jnp.concatenate([a[:, own:], b[:, own:]], axis=1)
        pieces.append(jnp.concatenate([top, low], axis=0))
    s = jnp.concatenate(pieces, axis=1)
    s1, s2 = (v.astype(BF16) for v in split(s, 2))
    width = s.shape[1]
    none = jnp.zeros((1, width), F32)
    akm[...] = jnp.concatenate([s1, s1, s2, vector_rows(none, None, width), jnp.zeros((16, width), BF16)], axis=0)
    copies[0].wait()
    weights = jnp.concatenate([la[...] * LOG2E, jnp.zeros_like(la[...])], axis=1)
    out[:, :, width:] = jnp.broadcast_to(weights[None], (out.shape[0], 1, 2 * own))
    width = 2 * tpg.shape[2]
    none = jnp.zeros((1, width), F32)
    zeros = jnp.zeros((16, width), BF16)
    for p in range(tpg.shape[0]):
        copies[p + 1].wait()
        at = slice(width * p, width * (p + 1))
        wide = lambda row, count: jnp.concatenate([tpg[p, row : row + count], tpg[p, row + count : row + 2 * count]], axis=1)
        t1, t2 = (v.astype(BF16) for v in split(wide(0, DIM), 2))
        h = wide(2 * DIM, 1)
        lb[:, at] = wide(2 * DIM + 2, 1)
        bkm[:, at] = jnp.concatenate([t1, t2, t1, vector_rows(None, none, width), zeros], axis=0)
        bh[:, at] = jnp.concatenate([t1, t2, t1, vector_rows(None, h, width), zeros], axis=0)
    lse_pass(bh, brm, akm, write_copies(out))


def first_column_kernel(parts, akm, bkm, out, la, arm, tmp):
    rows = la.shape[1]
    own = rows // parts.shape[0]
    for p in range(0, parts.shape[0], 2):
        la[:, own * p : own * (p + 2)] = jnp.concatenate(
            [parts[p, :, rows : rows + own], parts[p + 1, :, rows : rows + own]], axis=1
        )
    k = la[...] - combine(parts[:, :, :rows])
    tmp[...] = akm[...]
    tmp[VEC : VEC + 16, :] = vector_rows(k, None, k.shape[1])
    lse_pass(tmp, arm, bkm, write_dense(out))


def row_kernel(parts, lb, akm, bkm, out, brm, tmp):
    dense = combine(parts[...])
    h = lb[...] - jnp.concatenate([dense[r : r + 1] for r in range(dense.shape[0])], axis=1)
    tmp[...] = bkm[...]
    tmp[VEC : VEC + 16, :] = vector_rows(None, h, h.shape[1])
    lse_pass(tmp, brm, akm, write_copies(out))


def last_column_kernel(parts, la, akm, bkm, out, own_rows, arm, tmp):
    rows = combine(parts[...])
    me = lax.axis_index(TARGET_AXES)
    own = own_rows.shape[1]
    mine = jnp.zeros((1, own), F32)
    for p in range(rows.shape[1] // own):
        mine = mine + jnp.where(me == p, rows[:, own * p : own * (p + 1)], 0.0)
    own_rows[...] = mine
    k = la[...] - rows
    tmp[...] = akm[...]
    tmp[VEC : VEC + 16, :] = vector_rows(k, None, k.shape[1])

    def write(n, value):
        out[n] = value

    lse_pass(tmp, arm, bkm, write)


def last_kernel(parts, own_rows, ssq, tsq, f, g):
    f[...] = ssq[...] - (EPSILON * LN2) * own_rows[...]
    g[...] = tsq[...] - (EPSILON * LN2) * combine(parts[...])


def call(kernel, name, outs, *args, scratch=(), inputs=None, cost=None, vmem=48):
    whole = pl.BlockSpec(memory_space=pltpu.VMEM)
    return pl.pallas_call(
        kernel,
        name=name,
        out_shape=[jax.ShapeDtypeStruct(*o) for o in outs],
        in_specs=[pl.BlockSpec(memory_space=space) for space in inputs or [pltpu.VMEM] * len(args)],
        out_specs=[whole] * len(outs),
        scratch_shapes=list(scratch),
        compiler_params=pltpu.CompilerParams(vmem_limit_bytes=vmem << 20),
        cost_estimate=cost,
    )(*args)


def exchange(v, axes):
    return lax.all_to_all(v, axes, 0, 0, tiled=True)


def swap(v, axis, offset):
    size = lax.axis_size(axis)
    return lax.ppermute(v, axis, [(i, i ^ offset) for i in range(size)])


def pinned(*arrays):
    return [pltpu.with_memory_space_constraint(v, pltpu.HBM) for v in arrays]


def local(src_points, log_a, tgt_points, log_b, g_init):
    own_s, own_t = src_points.shape[0], tgt_points.shape[0]
    across_t = lax.axis_size(TARGET_AXES)
    across_s = lax.axis_size(SOURCE_AXES)
    rows, cols = own_s * across_t, own_t * across_s
    row = lambda v: v.reshape(1, -1)
    spack, tpack, ssq, tsq = call(
        pack_kernel,
        "pack",
        [
            ((DIM // 2, 2 * own_s), F32),
            ((across_s, 2 * DIM + 8, own_t // 2), F32),
            ((1, own_s), F32),
            ((1, own_t), F32),
        ],
        *pinned(src_points.T, tgt_points.T, row(log_b), row(g_init)),
        scratch=[pltpu.VMEM((DIM, own_s), F32), pltpu.VMEM((DIM, own_t), F32)]
        + [pltpu.VMEM((1, own_t), F32)] * 2
        + [pltpu.SemaphoreType.DMA((4,))],
        inputs=[pltpu.HBM] * 4,
        vmem=8,
    )
    pair = call(
        join_kernel, "join", [((DIM, 2 * own_s), F32)], spack, swap(spack, "z", 4), cost=JOIN_COST, vmem=2
    )[0]
    mine = jnp.concatenate([pair] + [swap(pair, "z", k) for k in (1, 2, 3)], axis=0)
    groups = [mine, swap(mine, "c", 1)]
    tpg = exchange(tpack, SOURCE_AXES)
    row_out = ((across_t, 1, rows), F32)
    col_out = ((across_s, 8, cols // 8), F32)
    parts, akm, bkm, lb = call(
        first_kernel,
        "row_pass_first",
        [((across_t, 1, rows + 2 * own_s), F32), ((DEPTH, rows), BF16), ((DEPTH, cols), BF16), ((1, cols), F32)],
        *groups,
        *pinned(tpg, row(log_a)),
        scratch=[pltpu.VMEM((cols, DEPTH), BF16), pltpu.VMEM((DEPTH, cols), BF16)]
        + [pltpu.VMEM((across_t, DIM // 2, 2 * own_s), F32), pltpu.VMEM(tpg.shape, F32)]
        + [pltpu.VMEM((1, own_s), F32), pltpu.SemaphoreType.DMA((across_s + 1,))],
        inputs=[pltpu.VMEM] * 2 + [pltpu.HBM] * 2,
    )
    row_scratch = [pltpu.VMEM((cols, DEPTH), BF16), pltpu.VMEM((DEPTH, cols), BF16)]
    col_scratch = [pltpu.VMEM((rows, DEPTH), BF16), pltpu.VMEM((DEPTH, rows), BF16)]
    parts = exchange(parts, TARGET_AXES)
    parts, la = call(
        first_column_kernel, "column_pass", [col_out, ((1, rows), F32)], parts, akm, bkm, scratch=col_scratch
    )
    parts = exchange(parts, SOURCE_AXES)
    (parts,) = call(row_kernel, "row_pass", [row_out], parts, lb, akm, bkm, scratch=row_scratch)
    parts = exchange(parts, TARGET_AXES)
    parts, own_rows = call(
        last_column_kernel,
        "column_pass_last",
        [((across_s, 1, own_t), F32), ((1, own_s), F32)],
        parts,
        la,
        akm,
        bkm,
        scratch=col_scratch,
    )
    parts = exchange(parts, SOURCE_AXES)
    f, g = call(last_kernel, "last", [((1, own_s), F32), ((1, own_t), F32)], parts, own_rows, ssq, tsq)
    return f.reshape(own_s), g.reshape(own_t)


def solution(mesh):
    fine = Mesh(mesh.devices.reshape(4, 8, 4, 2), AXES)
    flat = P(AXES)
    return jax.shard_map(
        local,
        mesh=fine,
        in_specs=(P(AXES, None), flat, P(AXES, None), flat, flat),
        out_specs=(flat, flat),
        check_vma=False,
    )
```

```python
import jax
import jax.numpy as jnp
import numpy as np
from jax import lax
from jax.experimental import pallas as pl
from jax.experimental.pallas import tpu as pltpu
from jax.sharding import Mesh
from jax.sharding import PartitionSpec as P

EPSILON = 0.5
LOG2E = float(np.log2(np.e))
LN2 = float(np.log(2.0))
AXES = ("x", "z", "y", "c")
SOURCE_AXES = ("y", "x")
TARGET_AXES = ("c", "z")
DIM = 32
PACK = DIM // 2 + 8
DEPTH = 128
VEC = 3 * DIM
TILE = 256
CHUNK = 128
OVERFLOW = 1e38
F32 = jnp.float32
BF16 = jnp.bfloat16
Z_ORDER = (0, 4, 1, 5, 2, 6, 3, 7)
JOIN_COST = pl.CostEstimate(flops=1000000000000, bytes_accessed=0, transcendentals=0)


def split(v, count):
    pieces = []
    for _ in range(count):
        piece = v.astype(BF16)
        pieces.append(piece.astype(F32))
        v = v - pieces[-1]
    return pieces


def vector_rows(first, second, width):
    def rows(v):
        if v is None:
            return [jnp.ones((1, width), F32)] * 3
        return split(v, 3)

    zeros = jnp.zeros((10, width), F32)
    return jnp.concatenate(rows(first) + rows(second) + [zeros], axis=0).astype(BF16)


def flat(dense):
    return jnp.concatenate([dense[r : r + 1] for r in range(dense.shape[0])], axis=1)


def combine(parts):
    top = jnp.max(parts, axis=0)
    return top + jnp.log2(jnp.sum(jnp.exp2(parts - top[None]), axis=0))


def lse_pass(lhs_t, lhs_ref, rhs_ref, write):
    largest = None
    for at in range(0, rhs_ref.shape[1], TILE):
        rhs = rhs_ref[:, at : at + TILE]
        top = total = None
        for row in range(0, lhs_ref.shape[0], CHUNK):
            if at == 0:
                lhs = lhs_t[:, row : row + CHUNK].T
                lhs_ref[row : row + CHUNK, :] = lhs
            else:
                lhs = lhs_ref[row : row + CHUNK, :]
            terms = jnp.dot(lhs, rhs, preferred_element_type=F32).reshape(CHUNK // 8, 8, TILE)
            if top is None:
                top = jnp.max(jnp.max(terms, axis=0), axis=0, keepdims=True)
            added = jnp.sum(jnp.exp2(terms - top[None]), axis=0)
            total = added if total is None else total + added
        total = jnp.sum(total, axis=0, keepdims=True)
        largest = total if largest is None else jnp.maximum(largest, total)
        write(at // TILE, top + jnp.log2(total))

    @pl.when(jnp.logical_not(jnp.max(largest) < OVERFLOW))
    def _():
        running_lse_pass(lhs_ref, rhs_ref, write)


def running_lse_pass(lhs_ref, rhs_ref, write):
    def tile(n, carry):
        rhs = rhs_ref[:, pl.ds(pl.multiple_of(n * TILE, TILE), TILE)]

        def step(r, state):
            top, total = state
            lhs = lhs_ref[pl.ds(pl.multiple_of(r * CHUNK, CHUNK), CHUNK), :]
            terms = jnp.dot(lhs, rhs, preferred_element_type=F32).reshape(CHUNK // 8, 8, TILE)
            newtop = jnp.maximum(top, jnp.max(terms, axis=0))
            added = jnp.sum(jnp.exp2(terms - newtop[None]), axis=0)
            return newtop, total * jnp.exp2(top - newtop) + added

        start = (jnp.full((8, TILE), -1e30, F32), jnp.zeros((8, TILE), F32))
        top, total = lax.fori_loop(0, lhs_ref.shape[0] // CHUNK, step, start, unroll=8)
        peak = jnp.max(top, axis=0, keepdims=True)
        total = jnp.sum(total * jnp.exp2(top - peak), axis=0, keepdims=True)
        write(n, peak + jnp.log2(total))
        return carry

    lax.fori_loop(0, rhs_ref.shape[1] // TILE, tile, 0)


def write_dense(out_ref):
    copies, _, width = out_ref.shape
    step = min(TILE, width)

    def write(n, value):
        for at in range(0, TILE, step):
            start = n * TILE + at
            row, lane = start // width, start % width
            lane = lane if isinstance(n, int) else pl.multiple_of(lane, step)
            piece = value[None, :, at : at + step]
            out_ref[:, pl.ds(row, 1), pl.ds(lane, step)] = jnp.broadcast_to(piece, (copies, 1, step))

    return write


def pack_kernel(src_hbm, la_hbm, tgt_hbm, lb_hbm, g_hbm, spack, tpack, ssq, tsq, src, la, tgt, lb, g, sems):
    pairs = ((src_hbm, src), (la_hbm, la), (tgt_hbm, tgt), (lb_hbm, lb), (g_hbm, g))
    copies = [pltpu.make_async_copy(a, b, sems.at[i]) for i, (a, b) in enumerate(pairs)]
    for copy in copies:
        copy.start()
    for copy in copies:
        copy.wait()
    s_t, t_t = src[...], tgt[...]
    s_norm = jnp.sum(s_t * s_t, axis=0, keepdims=True)
    t_norm = jnp.sum(t_t * t_t, axis=0, keepdims=True)
    ssq[...] = s_norm
    tsq[...] = t_norm
    s_t = s_t * ((2.0 / EPSILON) * LOG2E)
    weights = jnp.concatenate([la[...] * LOG2E, jnp.zeros_like(la[...])], axis=1)
    spack[: DIM // 2] = jnp.concatenate([s_t[: DIM // 2], s_t[DIM // 2 :]], axis=1)
    spack[DIM // 2 :] = jnp.broadcast_to(weights, (PACK - DIM // 2, weights.shape[1]))
    h = (lb[...] + (g[...] - t_norm) / EPSILON) * LOG2E
    weights = lb[...] * LOG2E
    half = t_t.shape[1] // 2
    rows = [t_t[:, :half], t_t[:, half:], h[:, :half], h[:, half:], weights[:, :half], weights[:, half:]]
    packed = jnp.concatenate(rows + [jnp.zeros((4, half), F32)], axis=0)
    tpack[...] = jnp.broadcast_to(packed[None], tpack.shape)


def join_kernel(first, second, out):
    rows = first.shape[0]
    out[:rows] = first[...]
    out[rows:] = second[...]


def first_kernel(mine, other, tpg_hbm, out, akm, bkm, la, lb, brm, bh, packs, tpg, sem):
    copy = pltpu.make_async_copy(tpg_hbm, tpg, sem)
    copy.start()
    own = mine.shape[1] // 2
    half = DIM // 2
    me = lax.axis_index(TARGET_AXES)
    for at, offset in enumerate(Z_ORDER):
        row = slice(PACK * at, PACK * (at + 1))
        packs[offset], packs[offset + 8] = mine[row], other[row]
    pieces = []
    for p in range(0, packs.shape[0], 2):
        a, b = packs[p ^ me], packs[(p + 1) ^ me]
        top = jnp.concatenate([a[:, :own], b[:, :own]], axis=1)
        low = jnp.concatenate([a[:half, own:], b[:half, own:]], axis=1)
        la[:, own * p : own * (p + 2)] = top[half : half + 1]
        pieces.append(jnp.concatenate([top[:half], low], axis=0))
    s = jnp.concatenate(pieces, axis=1)
    s1, s2 = (v.astype(BF16) for v in split(s, 2))
    width = s.shape[1]
    none = jnp.zeros((1, width), F32)
    akm[...] = jnp.concatenate([s1, s1, s2, vector_rows(none, None, width), jnp.zeros((16, width), BF16)], axis=0)
    copy.wait()
    width = 2 * tpg.shape[2]
    none = jnp.zeros((1, width), F32)
    zeros = jnp.zeros((16, width), BF16)
    for p in range(tpg.shape[0]):
        at = slice(width * p, width * (p + 1))
        wide = lambda row, count: jnp.concatenate([tpg[p, row : row + count], tpg[p, row + count : row + 2 * count]], axis=1)
        t1, t2 = (v.astype(BF16) for v in split(wide(0, DIM), 2))
        h = wide(2 * DIM, 1)
        lb[:, at] = wide(2 * DIM + 2, 1)
        bkm[:, at] = jnp.concatenate([t1, t2, t1, vector_rows(None, none, width), zeros], axis=0)
        bh[:, at] = jnp.concatenate([t1, t2, t1, vector_rows(None, h, width), zeros], axis=0)
    lse_pass(bh, brm, akm, write_dense(out))


def column_kernel(parts, la, akm, bkm, out, arm, tmp):
    k = la[...] - flat(combine(parts[...]))
    tmp[...] = akm[...]
    tmp[VEC : VEC + 16, :] = vector_rows(k, None, k.shape[1])
    lse_pass(tmp, arm, bkm, write_dense(out))


def row_kernel(parts, lb, akm, bkm, out, brm, tmp):
    h = lb[...] - flat(combine(parts[...]))
    tmp[...] = bkm[...]
    tmp[VEC : VEC + 16, :] = vector_rows(None, h, h.shape[1])
    lse_pass(tmp, brm, akm, write_dense(out))


def last_column_kernel(parts, la, akm, bkm, out, own_rows, arm, tmp):
    rows = flat(combine(parts[...]))
    me = lax.axis_index(TARGET_AXES)
    own = own_rows.shape[1]
    mine = jnp.zeros((1, own), F32)
    for p in range(rows.shape[1] // own):
        mine = mine + jnp.where(me == p, rows[:, own * p : own * (p + 1)], 0.0)
    own_rows[...] = mine
    k = la[...] - rows
    tmp[...] = akm[...]
    tmp[VEC : VEC + 16, :] = vector_rows(k, None, k.shape[1])

    def write(n, value):
        out[n] = value

    lse_pass(tmp, arm, bkm, write)


def last_kernel(parts, own_rows, ssq, tsq, f, g):
    f[...] = ssq[...] - (EPSILON * LN2) * own_rows[...]
    g[...] = tsq[...] - (EPSILON * LN2) * combine(parts[...])


def call(kernel, name, outs, *args, scratch=(), inputs=None, cost=None, vmem=48):
    whole = pl.BlockSpec(memory_space=pltpu.VMEM)
    return pl.pallas_call(
        kernel,
        name=name,
        out_shape=[jax.ShapeDtypeStruct(*o) for o in outs],
        in_specs=[pl.BlockSpec(memory_space=space) for space in inputs or [pltpu.VMEM] * len(args)],
        out_specs=[whole] * len(outs),
        scratch_shapes=list(scratch),
        compiler_params=pltpu.CompilerParams(vmem_limit_bytes=vmem << 20),
        cost_estimate=cost,
    )(*args)


def exchange(v, axes):
    return lax.all_to_all(v, axes, 0, 0, tiled=True)


def swap(v, axis, offset):
    size = lax.axis_size(axis)
    return lax.ppermute(v, axis, [(i, i ^ offset) for i in range(size)])


def pinned(*arrays):
    return [pltpu.with_memory_space_constraint(v, pltpu.HBM) for v in arrays]


def local(src_points, log_a, tgt_points, log_b, g_init):
    own_s, own_t = src_points.shape[0], tgt_points.shape[0]
    across_t = lax.axis_size(TARGET_AXES)
    across_s = lax.axis_size(SOURCE_AXES)
    rows, cols = own_s * across_t, own_t * across_s
    row = lambda v: v.reshape(1, -1)
    spack, tpack, ssq, tsq = call(
        pack_kernel,
        "pack",
        [
            ((PACK, 2 * own_s), F32),
            ((across_s, 2 * DIM + 8, own_t // 2), F32),
            ((1, own_s), F32),
            ((1, own_t), F32),
        ],
        *pinned(src_points.T, row(log_a), tgt_points.T, row(log_b), row(g_init)),
        scratch=[pltpu.VMEM((DIM, own_s), F32), pltpu.VMEM((1, own_s), F32), pltpu.VMEM((DIM, own_t), F32)]
        + [pltpu.VMEM((1, own_t), F32)] * 2
        + [pltpu.SemaphoreType.DMA((5,))],
        inputs=[pltpu.HBM] * 5,
        vmem=8,
    )
    pair = call(
        join_kernel, "join", [((2 * PACK, 2 * own_s), F32)], spack, swap(spack, "z", 4), cost=JOIN_COST, vmem=2
    )[0]
    mine = jnp.concatenate([pair] + [swap(pair, "z", k) for k in (1, 2, 3)], axis=0)
    groups = [mine, swap(mine, "c", 1)]
    tpg = exchange(tpack, SOURCE_AXES)
    row_out = ((across_t, 8, rows // 8), F32)
    col_out = ((across_s, 8, cols // 8), F32)
    parts, akm, bkm, la, lb = call(
        first_kernel,
        "row_pass_first",
        [row_out, ((DEPTH, rows), BF16), ((DEPTH, cols), BF16), ((1, rows), F32), ((1, cols), F32)],
        *groups,
        *pinned(tpg),
        scratch=[pltpu.VMEM((cols, DEPTH), BF16), pltpu.VMEM((DEPTH, cols), BF16)]
        + [pltpu.VMEM((across_t, PACK, 2 * own_s), F32), pltpu.VMEM(tpg.shape, F32)]
        + [pltpu.SemaphoreType.DMA],
        inputs=[pltpu.VMEM] * 2 + [pltpu.HBM],
    )
    row_scratch = [pltpu.VMEM((cols, DEPTH), BF16), pltpu.VMEM((DEPTH, cols), BF16)]
    col_scratch = [pltpu.VMEM((rows, DEPTH), BF16), pltpu.VMEM((DEPTH, rows), BF16)]
    parts = exchange(parts, TARGET_AXES)
    (parts,) = call(column_kernel, "column_pass", [col_out], parts, la, akm, bkm, scratch=col_scratch)
    parts = exchange(parts, SOURCE_AXES)
    (parts,) = call(row_kernel, "row_pass", [row_out], parts, lb, akm, bkm, scratch=row_scratch)
    parts = exchange(parts, TARGET_AXES)
    parts, own_rows = call(
        last_column_kernel,
        "column_pass_last",
        [((across_s, 1, own_t), F32), ((1, own_s), F32)],
        parts,
        la,
        akm,
        bkm,
        scratch=col_scratch,
    )
    parts = exchange(parts, SOURCE_AXES)
    f, g = call(last_kernel, "last", [((1, own_s), F32), ((1, own_t), F32)], parts, own_rows, ssq, tsq)
    return f.reshape(own_s), g.reshape(own_t)


def solution(mesh):
    fine = Mesh(mesh.devices.reshape(4, 8, 4, 2), AXES)
    flat = P(AXES)
    return jax.shard_map(
        local,
        mesh=fine,
        in_specs=(P(AXES, None), flat, P(AXES, None), flat, flat),
        out_specs=(flat, flat),
        check_vma=False,
    )
```

```python
import jax
import jax.numpy as jnp
import numpy as np
from jax import lax
from jax.experimental import pallas as pl
from jax.experimental.pallas import tpu as pltpu
from jax.sharding import Mesh
from jax.sharding import PartitionSpec as P

EPSILON = 0.5
LOG2E = float(np.log2(np.e))
LN2 = float(np.log(2.0))
Z = ("z2", "z1", "z0")
AXES = ("x", *Z, "y", "c")
SOURCE_AXES = ("y", "x")
TARGET_AXES = ("c", "z1", "z2", "z0")
DIM = 32
PACK = DIM // 2 + 8
DEPTH = 128
VEC = 3 * DIM
TILE = 256
CHUNK = 128
OVERFLOW = 1e38
F32 = jnp.float32
BF16 = jnp.bfloat16
Z_ORDER = (0, 2, 1, 3, 4, 6, 5, 7)
JOIN_COST = pl.CostEstimate(flops=1000000000000, bytes_accessed=0, transcendentals=0)


def split(v, count):
    pieces = []
    for _ in range(count):
        piece = v.astype(BF16)
        pieces.append(piece.astype(F32))
        v = v - pieces[-1]
    return pieces


def vector_rows(first, second, width):
    def rows(v):
        if v is None:
            return [jnp.ones((1, width), F32)] * 3
        return split(v, 3)

    zeros = jnp.zeros((10, width), F32)
    return jnp.concatenate(rows(first) + rows(second) + [zeros], axis=0).astype(BF16)


def flat(dense):
    return jnp.concatenate([dense[r : r + 1] for r in range(dense.shape[0])], axis=1)


def combine(parts):
    top = jnp.max(parts, axis=0)
    return top + jnp.log2(jnp.sum(jnp.exp2(parts - top[None]), axis=0))


def lse_pass(lhs_t, lhs_ref, rhs_ref, write):
    largest = None
    for at in range(0, rhs_ref.shape[1], TILE):
        rhs = rhs_ref[:, at : at + TILE]
        top = total = None
        for row in range(0, lhs_ref.shape[0], CHUNK):
            if at == 0:
                lhs = lhs_t[:, row : row + CHUNK].T
                lhs_ref[row : row + CHUNK, :] = lhs
            else:
                lhs = lhs_ref[row : row + CHUNK, :]
            terms = jnp.dot(lhs, rhs, preferred_element_type=F32).reshape(CHUNK // 8, 8, TILE)
            if top is None:
                top = jnp.max(jnp.max(terms, axis=0), axis=0, keepdims=True)
            added = jnp.sum(jnp.exp2(terms - top[None]), axis=0)
            total = added if total is None else total + added
        total = jnp.sum(total, axis=0, keepdims=True)
        largest = total if largest is None else jnp.maximum(largest, total)
        write(at // TILE, top + jnp.log2(total))

    @pl.when(jnp.logical_not(jnp.max(largest) < OVERFLOW))
    def _():
        running_lse_pass(lhs_ref, rhs_ref, write)


def running_lse_pass(lhs_ref, rhs_ref, write):
    def tile(n, carry):
        rhs = rhs_ref[:, pl.ds(pl.multiple_of(n * TILE, TILE), TILE)]

        def step(r, state):
            top, total = state
            lhs = lhs_ref[pl.ds(pl.multiple_of(r * CHUNK, CHUNK), CHUNK), :]
            terms = jnp.dot(lhs, rhs, preferred_element_type=F32).reshape(CHUNK // 8, 8, TILE)
            newtop = jnp.maximum(top, jnp.max(terms, axis=0))
            added = jnp.sum(jnp.exp2(terms - newtop[None]), axis=0)
            return newtop, total * jnp.exp2(top - newtop) + added

        start = (jnp.full((8, TILE), -1e30, F32), jnp.zeros((8, TILE), F32))
        top, total = lax.fori_loop(0, lhs_ref.shape[0] // CHUNK, step, start, unroll=8)
        peak = jnp.max(top, axis=0, keepdims=True)
        total = jnp.sum(total * jnp.exp2(top - peak), axis=0, keepdims=True)
        write(n, peak + jnp.log2(total))
        return carry

    lax.fori_loop(0, rhs_ref.shape[1] // TILE, tile, 0)


def write_dense(out_ref):
    copies, _, width = out_ref.shape
    step = min(TILE, width)

    def write(n, value):
        for at in range(0, TILE, step):
            start = n * TILE + at
            row, lane = start // width, start % width
            lane = lane if isinstance(n, int) else pl.multiple_of(lane, step)
            piece = value[None, :, at : at + step]
            out_ref[:, pl.ds(row, 1), pl.ds(lane, step)] = jnp.broadcast_to(piece, (copies, 1, step))

    return write


def pack_kernel(src_hbm, la_hbm, tgt_hbm, lb_hbm, g_hbm, spack, tpack, ssq, tsq, src, la, tgt, lb, g, sems):
    pairs = ((src_hbm, src), (la_hbm, la), (tgt_hbm, tgt), (lb_hbm, lb), (g_hbm, g))
    copies = [pltpu.make_async_copy(a, b, sems.at[i]) for i, (a, b) in enumerate(pairs)]
    for copy in copies:
        copy.start()
    for copy in copies:
        copy.wait()
    s_t, t_t = src[...], tgt[...]
    s_norm = jnp.sum(s_t * s_t, axis=0, keepdims=True)
    t_norm = jnp.sum(t_t * t_t, axis=0, keepdims=True)
    ssq[...] = s_norm
    tsq[...] = t_norm
    s_t = s_t * ((2.0 / EPSILON) * LOG2E)
    weights = jnp.concatenate([la[...] * LOG2E, jnp.zeros_like(la[...])], axis=1)
    spack[: DIM // 2] = jnp.concatenate([s_t[: DIM // 2], s_t[DIM // 2 :]], axis=1)
    spack[DIM // 2 :] = jnp.broadcast_to(weights, (PACK - DIM // 2, weights.shape[1]))
    h = (lb[...] + (g[...] - t_norm) / EPSILON) * LOG2E
    weights = lb[...] * LOG2E
    half = t_t.shape[1] // 2
    rows = [t_t[:, :half], t_t[:, half:], h[:, :half], h[:, half:], weights[:, :half], weights[:, half:]]
    packed = jnp.concatenate(rows + [jnp.zeros((4, half), F32)], axis=0)
    tpack[...] = jnp.broadcast_to(packed[None], tpack.shape)


def join_kernel(first, second, out):
    rows = first.shape[0]
    out[:rows] = first[...]
    out[rows:] = second[...]


def first_kernel(mine, other, tpg_hbm, out, akm, bkm, la, lb, brm, bh, packs, tpg, sem):
    copy = pltpu.make_async_copy(tpg_hbm, tpg, sem)
    copy.start()
    own = mine.shape[1] // 2
    half = DIM // 2
    me = lax.axis_index(TARGET_AXES)
    for at, offset in enumerate(Z_ORDER):
        row = slice(PACK * at, PACK * (at + 1))
        packs[offset], packs[offset + 8] = mine[row], other[row]
    pieces = []
    for p in range(0, packs.shape[0], 2):
        a, b = packs[p ^ me], packs[(p + 1) ^ me]
        top = jnp.concatenate([a[:, :own], b[:, :own]], axis=1)
        low = jnp.concatenate([a[:half, own:], b[:half, own:]], axis=1)
        la[:, own * p : own * (p + 2)] = top[half : half + 1]
        pieces.append(jnp.concatenate([top[:half], low], axis=0))
    s = jnp.concatenate(pieces, axis=1)
    s1, s2 = (v.astype(BF16) for v in split(s, 2))
    width = s.shape[1]
    none = jnp.zeros((1, width), F32)
    akm[...] = jnp.concatenate([s1, s1, s2, vector_rows(none, None, width), jnp.zeros((16, width), BF16)], axis=0)
    copy.wait()
    width = 2 * tpg.shape[2]
    none = jnp.zeros((1, width), F32)
    zeros = jnp.zeros((16, width), BF16)
    for p in range(tpg.shape[0]):
        at = slice(width * p, width * (p + 1))
        wide = lambda row, count: jnp.concatenate([tpg[p, row : row + count], tpg[p, row + count : row + 2 * count]], axis=1)
        t1, t2 = (v.astype(BF16) for v in split(wide(0, DIM), 2))
        h = wide(2 * DIM, 1)
        lb[:, at] = wide(2 * DIM + 2, 1)
        bkm[:, at] = jnp.concatenate([t1, t2, t1, vector_rows(None, none, width), zeros], axis=0)
        bh[:, at] = jnp.concatenate([t1, t2, t1, vector_rows(None, h, width), zeros], axis=0)
    lse_pass(bh, brm, akm, write_dense(out))


def column_kernel(parts, la, akm, bkm, out, arm, tmp):
    k = la[...] - flat(combine(parts[...]))
    tmp[...] = akm[...]
    tmp[VEC : VEC + 16, :] = vector_rows(k, None, k.shape[1])
    lse_pass(tmp, arm, bkm, write_dense(out))


def row_kernel(parts, lb, akm, bkm, out, brm, tmp):
    h = lb[...] - flat(combine(parts[...]))
    tmp[...] = bkm[...]
    tmp[VEC : VEC + 16, :] = vector_rows(None, h, h.shape[1])
    lse_pass(tmp, brm, akm, write_dense(out))


def last_column_kernel(parts, la, akm, bkm, out, own_rows, arm, tmp):
    rows = flat(combine(parts[...]))
    me = lax.axis_index(TARGET_AXES)
    own = own_rows.shape[1]
    mine = jnp.zeros((1, own), F32)
    for p in range(rows.shape[1] // own):
        mine = mine + jnp.where(me == p, rows[:, own * p : own * (p + 1)], 0.0)
    own_rows[...] = mine
    k = la[...] - rows
    tmp[...] = akm[...]
    tmp[VEC : VEC + 16, :] = vector_rows(k, None, k.shape[1])

    def write(n, value):
        out[n] = value

    lse_pass(tmp, arm, bkm, write)


def last_kernel(parts, own_rows, ssq, tsq, f, g):
    f[...] = ssq[...] - (EPSILON * LN2) * own_rows[...]
    g[...] = tsq[...] - (EPSILON * LN2) * combine(parts[...])


def call(kernel, name, outs, *args, scratch=(), inputs=None, cost=None, vmem=48):
    whole = pl.BlockSpec(memory_space=pltpu.VMEM)
    return pl.pallas_call(
        kernel,
        name=name,
        out_shape=[jax.ShapeDtypeStruct(*o) for o in outs],
        in_specs=[pl.BlockSpec(memory_space=space) for space in inputs or [pltpu.VMEM] * len(args)],
        out_specs=[whole] * len(outs),
        scratch_shapes=list(scratch),
        compiler_params=pltpu.CompilerParams(vmem_limit_bytes=vmem << 20),
        cost_estimate=cost,
    )(*args)


def exchange(v, axes):
    return lax.all_to_all(v, axes, 0, 0, tiled=True)


def swap(v, axis, offset):
    size = lax.axis_size(axis)
    return lax.ppermute(v, axis, [(i, i ^ offset) for i in range(size)])


def pinned(*arrays):
    return [pltpu.with_memory_space_constraint(v, pltpu.HBM) for v in arrays]


def local(src_points, log_a, tgt_points, log_b, g_init):
    own_s, own_t = src_points.shape[0], tgt_points.shape[0]
    across_t = lax.axis_size(TARGET_AXES)
    across_s = lax.axis_size(SOURCE_AXES)
    rows, cols = own_s * across_t, own_t * across_s
    row = lambda v: v.reshape(1, -1)
    spack, tpack, ssq, tsq = call(
        pack_kernel,
        "pack",
        [
            ((PACK, 2 * own_s), F32),
            ((across_s, 2 * DIM + 8, own_t // 2), F32),
            ((1, own_s), F32),
            ((1, own_t), F32),
        ],
        *pinned(src_points.T, row(log_a), tgt_points.T, row(log_b), row(g_init)),
        scratch=[pltpu.VMEM((DIM, own_s), F32), pltpu.VMEM((1, own_s), F32), pltpu.VMEM((DIM, own_t), F32)]
        + [pltpu.VMEM((1, own_t), F32)] * 2
        + [pltpu.SemaphoreType.DMA((5,))],
        inputs=[pltpu.HBM] * 5,
        vmem=8,
    )
    pair = call(
        join_kernel, "join", [((2 * PACK, 2 * own_s), F32)], spack, swap(spack, Z, 4), cost=JOIN_COST, vmem=2
    )[0]
    mine = jnp.concatenate([pair] + [swap(pair, Z, k) for k in (1, 2, 3)], axis=0)
    groups = [mine, swap(mine, "c", 1)]
    tpg = exchange(tpack, SOURCE_AXES)
    row_out = ((across_t, 8, rows // 8), F32)
    col_out = ((across_s, 8, cols // 8), F32)
    parts, akm, bkm, la, lb = call(
        first_kernel,
        "row_pass_first",
        [row_out, ((DEPTH, rows), BF16), ((DEPTH, cols), BF16), ((1, rows), F32), ((1, cols), F32)],
        *groups,
        *pinned(tpg),
        scratch=[pltpu.VMEM((cols, DEPTH), BF16), pltpu.VMEM((DEPTH, cols), BF16)]
        + [pltpu.VMEM((across_t, PACK, 2 * own_s), F32), pltpu.VMEM(tpg.shape, F32)]
        + [pltpu.SemaphoreType.DMA],
        inputs=[pltpu.VMEM] * 2 + [pltpu.HBM],
    )
    row_scratch = [pltpu.VMEM((cols, DEPTH), BF16), pltpu.VMEM((DEPTH, cols), BF16)]
    col_scratch = [pltpu.VMEM((rows, DEPTH), BF16), pltpu.VMEM((DEPTH, rows), BF16)]
    parts = exchange(parts, TARGET_AXES)
    (parts,) = call(column_kernel, "column_pass", [col_out], parts, la, akm, bkm, scratch=col_scratch)
    parts = exchange(parts, SOURCE_AXES)
    (parts,) = call(row_kernel, "row_pass", [row_out], parts, lb, akm, bkm, scratch=row_scratch)
    parts = exchange(parts, TARGET_AXES)
    parts, own_rows = call(
        last_column_kernel,
        "column_pass_last",
        [((across_s, 1, own_t), F32), ((1, own_s), F32)],
        parts,
        la,
        akm,
        bkm,
        scratch=col_scratch,
    )
    parts = exchange(parts, SOURCE_AXES)
    f, g = call(last_kernel, "last", [((1, own_s), F32), ((1, own_t), F32)], parts, own_rows, ssq, tsq)
    return f.reshape(own_s), g.reshape(own_t)


def solution(mesh):
    fine = Mesh(mesh.devices.reshape(4, 2, 2, 2, 4, 2), AXES)
    flat = P(AXES)
    return jax.shard_map(
        local,
        mesh=fine,
        in_specs=(P(AXES, None), flat, P(AXES, None), flat, flat),
        out_specs=(flat, flat),
        check_vma=False,
    )
```

```python
import jax
import jax.numpy as jnp
import numpy as np
from jax import lax
from jax.experimental import pallas as pl
from jax.experimental.pallas import tpu as pltpu
from jax.sharding import Mesh
from jax.sharding import PartitionSpec as P

EPSILON = 0.5
LOG2E = float(np.log2(np.e))
LN2 = float(np.log(2.0))
AXES = ("x", "z", "y", "c")
SOURCE_AXES = ("y", "x")
TARGET_AXES = ("c", "z")
DIM = 32
PACK = DIM // 2 + 8
DEPTH = 128
VEC = 3 * DIM
TILE = 256
CHUNK = 128
OVERFLOW = 1e38
F32 = jnp.float32
BF16 = jnp.bfloat16
Z_ORDER = (0, 4, 1, 5, 2, 6, 3, 7)
JOIN_COST = pl.CostEstimate(flops=1000000000000, bytes_accessed=0, transcendentals=0)


def split(v, count):
    pieces = []
    for _ in range(count):
        piece = v.astype(BF16)
        pieces.append(piece.astype(F32))
        v = v - pieces[-1]
    return pieces


def vector_rows(first, second, width):
    def rows(v):
        if v is None:
            return [jnp.ones((1, width), F32)] * 3
        return split(v, 3)

    zeros = jnp.zeros((10, width), F32)
    return jnp.concatenate(rows(first) + rows(second) + [zeros], axis=0).astype(BF16)


def flat(dense):
    return jnp.concatenate([dense[r : r + 1] for r in range(dense.shape[0])], axis=1)


def combine(parts):
    top = jnp.max(parts, axis=0)
    return top + jnp.log2(jnp.sum(jnp.exp2(parts - top[None]), axis=0))


def lse_pass(lhs_t, lhs_ref, rhs_ref, write):
    largest = None
    for at in range(0, rhs_ref.shape[1], TILE):
        rhs = rhs_ref[:, at : at + TILE]
        top = total = None
        size = CHUNK if at == 0 or lhs_ref.shape[0] < rhs_ref.shape[1] else CHUNK // 2
        for row in range(0, lhs_ref.shape[0], size):
            if at == 0:
                lhs = lhs_t[:, row : row + CHUNK].T
                lhs_ref[row : row + CHUNK, :] = lhs
            else:
                lhs = lhs_ref[row : row + size, :]
            terms = jnp.dot(lhs, rhs, preferred_element_type=F32).reshape(size // 8, 8, TILE)
            if top is None:
                top = jnp.max(jnp.max(terms, axis=0), axis=0, keepdims=True)
            added = jnp.sum(jnp.exp2(terms - top[None]), axis=0)
            total = added if total is None else total + added
        total = jnp.sum(total, axis=0, keepdims=True)
        largest = total if largest is None else jnp.maximum(largest, total)
        write(at // TILE, top + jnp.log2(total))

    @pl.when(jnp.logical_not(jnp.max(largest) < OVERFLOW))
    def _():
        running_lse_pass(lhs_ref, rhs_ref, write)


def running_lse_pass(lhs_ref, rhs_ref, write):
    def tile(n, carry):
        rhs = rhs_ref[:, pl.ds(pl.multiple_of(n * TILE, TILE), TILE)]

        def step(r, state):
            top, total = state
            lhs = lhs_ref[pl.ds(pl.multiple_of(r * CHUNK, CHUNK), CHUNK), :]
            terms = jnp.dot(lhs, rhs, preferred_element_type=F32).reshape(CHUNK // 8, 8, TILE)
            newtop = jnp.maximum(top, jnp.max(terms, axis=0))
            added = jnp.sum(jnp.exp2(terms - newtop[None]), axis=0)
            return newtop, total * jnp.exp2(top - newtop) + added

        start = (jnp.full((8, TILE), -1e30, F32), jnp.zeros((8, TILE), F32))
        top, total = lax.fori_loop(0, lhs_ref.shape[0] // CHUNK, step, start, unroll=8)
        peak = jnp.max(top, axis=0, keepdims=True)
        total = jnp.sum(total * jnp.exp2(top - peak), axis=0, keepdims=True)
        write(n, peak + jnp.log2(total))
        return carry

    lax.fori_loop(0, rhs_ref.shape[1] // TILE, tile, 0)


def write_dense(out_ref):
    copies, _, width = out_ref.shape
    step = min(TILE, width)

    def write(n, value):
        for at in range(0, TILE, step):
            start = n * TILE + at
            row, lane = start // width, start % width
            lane = lane if isinstance(n, int) else pl.multiple_of(lane, step)
            piece = value[None, :, at : at + step]
            out_ref[:, pl.ds(row, 1), pl.ds(lane, step)] = jnp.broadcast_to(piece, (copies, 1, step))

    return write


def pack_kernel(src_hbm, la_hbm, tgt_hbm, lb_hbm, g_hbm, spack, tpack, ssq, tsq, src, la, tgt, lb, g, sems):
    pairs = ((src_hbm, src), (la_hbm, la), (tgt_hbm, tgt), (lb_hbm, lb), (g_hbm, g))
    copies = [pltpu.make_async_copy(a, b, sems.at[i]) for i, (a, b) in enumerate(pairs)]
    for copy in copies:
        copy.start()
    for copy in copies:
        copy.wait()
    s_t, t_t = src[...], tgt[...]
    s_norm = jnp.sum(s_t * s_t, axis=0, keepdims=True)
    t_norm = jnp.sum(t_t * t_t, axis=0, keepdims=True)
    ssq[...] = s_norm
    tsq[...] = t_norm
    s_t = s_t * ((2.0 / EPSILON) * LOG2E)
    weights = jnp.concatenate([la[...] * LOG2E, jnp.zeros_like(la[...])], axis=1)
    spack[: DIM // 2] = jnp.concatenate([s_t[: DIM // 2], s_t[DIM // 2 :]], axis=1)
    spack[DIM // 2 :] = jnp.broadcast_to(weights, (PACK - DIM // 2, weights.shape[1]))
    h = (lb[...] + (g[...] - t_norm) / EPSILON) * LOG2E
    weights = lb[...] * LOG2E
    half = t_t.shape[1] // 2
    rows = [t_t[:, :half], t_t[:, half:], h[:, :half], h[:, half:], weights[:, :half], weights[:, half:]]
    packed = jnp.concatenate(rows + [jnp.zeros((4, half), F32)], axis=0)
    tpack[...] = jnp.broadcast_to(packed[None], tpack.shape)


def join_kernel(first, second, out):
    rows = first.shape[0]
    out[:rows] = first[...]
    out[rows:] = second[...]


def first_kernel(mine, other, tpg_hbm, out, akm, bkm, la, lb, brm, bh, packs, tpg, sem):
    copy = pltpu.make_async_copy(tpg_hbm, tpg, sem)
    copy.start()
    own = mine.shape[1] // 2
    half = DIM // 2
    me = lax.axis_index(TARGET_AXES)
    for at, offset in enumerate(Z_ORDER):
        row = slice(PACK * at, PACK * (at + 1))
        packs[offset], packs[offset + 8] = mine[row], other[row]
    pieces = []
    for p in range(0, packs.shape[0], 2):
        a, b = packs[p ^ me], packs[(p + 1) ^ me]
        top = jnp.concatenate([a[:, :own], b[:, :own]], axis=1)
        low = jnp.concatenate([a[:half, own:], b[:half, own:]], axis=1)
        la[:, own * p : own * (p + 2)] = top[half : half + 1]
        pieces.append(jnp.concatenate([top[:half], low], axis=0))
    s = jnp.concatenate(pieces, axis=1)
    s1, s2 = (v.astype(BF16) for v in split(s, 2))
    width = s.shape[1]
    none = jnp.zeros((1, width), F32)
    akm[...] = jnp.concatenate([s1, s1, s2, vector_rows(none, None, width), jnp.zeros((16, width), BF16)], axis=0)
    copy.wait()
    width = 2 * tpg.shape[2]
    none = jnp.zeros((1, width), F32)
    zeros = jnp.zeros((16, width), BF16)
    for p in range(tpg.shape[0]):
        at = slice(width * p, width * (p + 1))
        wide = lambda row, count: jnp.concatenate([tpg[p, row : row + count], tpg[p, row + count : row + 2 * count]], axis=1)
        t1, t2 = (v.astype(BF16) for v in split(wide(0, DIM), 2))
        h = wide(2 * DIM, 1)
        lb[:, at] = wide(2 * DIM + 2, 1)
        bkm[:, at] = jnp.concatenate([t1, t2, t1, vector_rows(None, none, width), zeros], axis=0)
        bh[:, at] = jnp.concatenate([t1, t2, t1, vector_rows(None, h, width), zeros], axis=0)
    lse_pass(bh, brm, akm, write_dense(out))


def column_kernel(parts, la, akm, bkm, out, arm, tmp):
    k = la[...] - flat(combine(parts[...]))
    tmp[...] = akm[...]
    tmp[VEC : VEC + 16, :] = vector_rows(k, None, k.shape[1])
    lse_pass(tmp, arm, bkm, write_dense(out))


def row_kernel(parts, lb, akm, bkm, out, brm, tmp):
    h = lb[...] - flat(combine(parts[...]))
    tmp[...] = bkm[...]
    tmp[VEC : VEC + 16, :] = vector_rows(None, h, h.shape[1])
    lse_pass(tmp, brm, akm, write_dense(out))


def last_column_kernel(parts, la, akm, bkm, out, own_rows, arm, tmp):
    rows = flat(combine(parts[...]))
    me = lax.axis_index(TARGET_AXES)
    own = own_rows.shape[1]
    mine = jnp.zeros((1, own), F32)
    for p in range(rows.shape[1] // own):
        mine = mine + jnp.where(me == p, rows[:, own * p : own * (p + 1)], 0.0)
    own_rows[...] = mine
    k = la[...] - rows
    tmp[...] = akm[...]
    tmp[VEC : VEC + 16, :] = vector_rows(k, None, k.shape[1])

    def write(n, value):
        out[n] = value

    lse_pass(tmp, arm, bkm, write)


def last_kernel(parts, own_rows, ssq, tsq, f, g):
    f[...] = ssq[...] - (EPSILON * LN2) * own_rows[...]
    g[...] = tsq[...] - (EPSILON * LN2) * combine(parts[...])


def call(kernel, name, outs, *args, scratch=(), inputs=None, cost=None, vmem=48):
    whole = pl.BlockSpec(memory_space=pltpu.VMEM)
    return pl.pallas_call(
        kernel,
        name=name,
        out_shape=[jax.ShapeDtypeStruct(*o) for o in outs],
        in_specs=[pl.BlockSpec(memory_space=space) for space in inputs or [pltpu.VMEM] * len(args)],
        out_specs=[whole] * len(outs),
        scratch_shapes=list(scratch),
        compiler_params=pltpu.CompilerParams(vmem_limit_bytes=vmem << 20),
        cost_estimate=cost,
    )(*args)


def exchange(v, axes):
    return lax.all_to_all(v, axes, 0, 0, tiled=True)


def swap(v, axis, offset):
    size = lax.axis_size(axis)
    return lax.ppermute(v, axis, [(i, i ^ offset) for i in range(size)])


def pinned(*arrays):
    return [pltpu.with_memory_space_constraint(v, pltpu.HBM) for v in arrays]


def local(src_points, log_a, tgt_points, log_b, g_init):
    own_s, own_t = src_points.shape[0], tgt_points.shape[0]
    across_t = lax.axis_size(TARGET_AXES)
    across_s = lax.axis_size(SOURCE_AXES)
    rows, cols = own_s * across_t, own_t * across_s
    row = lambda v: v.reshape(1, -1)
    spack, tpack, ssq, tsq = call(
        pack_kernel,
        "pack",
        [
            ((PACK, 2 * own_s), F32),
            ((across_s, 2 * DIM + 8, own_t // 2), F32),
            ((1, own_s), F32),
            ((1, own_t), F32),
        ],
        *pinned(src_points.T, row(log_a), tgt_points.T, row(log_b), row(g_init)),
        scratch=[pltpu.VMEM((DIM, own_s), F32), pltpu.VMEM((1, own_s), F32), pltpu.VMEM((DIM, own_t), F32)]
        + [pltpu.VMEM((1, own_t), F32)] * 2
        + [pltpu.SemaphoreType.DMA((5,))],
        inputs=[pltpu.HBM] * 5,
        vmem=8,
    )
    pair = call(
        join_kernel, "join", [((2 * PACK, 2 * own_s), F32)], spack, swap(spack, "z", 4), cost=JOIN_COST, vmem=2
    )[0]
    mine = jnp.concatenate([pair] + [swap(pair, "z", k) for k in (1, 2, 3)], axis=0)
    groups = [mine, swap(mine, "c", 1)]
    tpg = exchange(tpack, SOURCE_AXES)
    row_out = ((across_t, 8, rows // 8), F32)
    col_out = ((across_s, 8, cols // 8), F32)
    parts, akm, bkm, la, lb = call(
        first_kernel,
        "row_pass_first",
        [row_out, ((DEPTH, rows), BF16), ((DEPTH, cols), BF16), ((1, rows), F32), ((1, cols), F32)],
        *groups,
        *pinned(tpg),
        scratch=[pltpu.VMEM((cols, DEPTH), BF16), pltpu.VMEM((DEPTH, cols), BF16)]
        + [pltpu.VMEM((across_t, PACK, 2 * own_s), F32), pltpu.VMEM(tpg.shape, F32)]
        + [pltpu.SemaphoreType.DMA],
        inputs=[pltpu.VMEM] * 2 + [pltpu.HBM],
    )
    row_scratch = [pltpu.VMEM((cols, DEPTH), BF16), pltpu.VMEM((DEPTH, cols), BF16)]
    col_scratch = [pltpu.VMEM((rows, DEPTH), BF16), pltpu.VMEM((DEPTH, rows), BF16)]
    parts = exchange(parts, TARGET_AXES)
    (parts,) = call(column_kernel, "column_pass", [col_out], parts, la, akm, bkm, scratch=col_scratch)
    parts = exchange(parts, SOURCE_AXES)
    (parts,) = call(row_kernel, "row_pass", [row_out], parts, lb, akm, bkm, scratch=row_scratch)
    parts = exchange(parts, TARGET_AXES)
    parts, own_rows = call(
        last_column_kernel,
        "column_pass_last",
        [((across_s, 1, own_t), F32), ((1, own_s), F32)],
        parts,
        la,
        akm,
        bkm,
        scratch=col_scratch,
    )
    parts = exchange(parts, SOURCE_AXES)
    f, g = call(last_kernel, "last", [((1, own_s), F32), ((1, own_t), F32)], parts, own_rows, ssq, tsq)
    return f.reshape(own_s), g.reshape(own_t)


def solution(mesh):
    fine = Mesh(mesh.devices.reshape(4, 8, 4, 2), AXES)
    flat = P(AXES)
    return jax.shard_map(
        local,
        mesh=fine,
        in_specs=(P(AXES, None), flat, P(AXES, None), flat, flat),
        out_specs=(flat, flat),
        check_vma=False,
    )
```
